128 devices in a mesh: row: 8 (over y, core), col: 16 (over x, z).
Axes of the slice: x: 4, y: 4, z: 4, core: 2. Of those that a mesh axis runs over, the one named last changes fastest.
Arguments:
- slab: float32 [65536, 8192], P(('row', 'col')), may hold values from -80 to 80, as said below
- sketch: float32 [8192, 128], replicated, may hold values from -0.0625 to 0.0625
Outputs:
- basis: float32 [65536, 128], P(('row', 'col'))
- projection: float32 [128, 8192], replicated
The draws below stay inside these ranges and needn't reach their ends.
Inputs may be any that keep to these rules, and one draw needn't show every extreme that they name: `slab`: each entry is one hidden-state value.
All inputs are finite; a program needn't handle non-finite values.
Results may differ from the reference program's by a relative error of at most 0.000084.
Values sent between devices are 32-bit elements; how exact they have to be, the bound alone decides.
No kernel may reach another device: no remote copies, remote signals or barrier semaphores. Data moves between devices by JAX's collectives and lax.ppermute only.
A program may use at most 128 MiB of HBM per device.

```python
import math
import jax
import jax.numpy as jnp
from jax import lax

D = 8192
K = 128
ROWS = 65536


def draw_slab(key, part):
    key = jax.random.fold_in(key, 11)
    key_noise, key_rows, key_cols = jax.random.split(key, 3)
    col_scale = jnp.exp(jax.random.uniform(key_cols, (1, D), jnp.float32, math.log(0.5), math.log(2.0)))
    noise = jnp.clip(jax.random.normal(key_noise, (ROWS, D), jnp.float32), -6.0, 6.0)
    row_scale = jnp.exp(jax.random.uniform(key_rows, (ROWS, 1), jnp.float32, 0.0, math.log(4.0)))
    return noise * row_scale * col_scale


def gaussian(own_key, extent, deviation, most, dtype=jnp.bfloat16):
    return jnp.clip(deviation * jax.random.normal(own_key, extent, jnp.float32), -most, most).astype(dtype)


def setup_inputs(seed: int = 0) -> dict:
    key_list = jax.random.split(jax.random.key(seed), 3)
    return {
        "slab": draw_slab(jax.random.fold_in(key_list[2], 71), 0),
        "sketch": gaussian(key_list[1], (D, K), D ** -0.5, 0.0625, jnp.float32),
    }


def reference(slab, sketch):
    highest = lax.Precision.HIGHEST
    sampled = jnp.dot(slab.astype(jnp.float32), sketch.astype(jnp.float32), precision=highest, preferred_element_type=jnp.float32)
    gram = jnp.dot(sampled.T, sampled, precision=highest)
    lower = jnp.linalg.cholesky(gram)
    transposed = jax.scipy.linalg.solve_triangular(lower, sampled.T, lower=True)
    basis = transposed.T * math.sqrt(ROWS)
    projection = jnp.dot(transposed, slab, precision=highest)
    return (basis, projection)
```

```python
import math

import jax
import jax.numpy as jnp
import numpy as np
from jax import lax
from jax.experimental import pallas as pl
from jax.experimental.pallas import tpu as pltpu
from jax.sharding import PartitionSpec as P

AXES = ("row", "col")
RING = 4
K = 128
CHUNK = 1024
SPLIT = (48, 40, 40)
STARTS = (0, 48, 88)
MIB = 2**20
F32 = jnp.float32
BF16 = jnp.bfloat16
HIGHEST = lax.Precision.HIGHEST


def places():
    return [
        (x, y, z, c) for y in range(RING) for c in range(2) for x in range(RING) for z in range(RING)
    ]


def linear(x, y, z, c):
    return (y * 2 + c) * RING * RING + x * RING + z


def beside(place, step, core):
    return place ^ 1 if (step ^ core) == 0 else RING - 1 - place


def ring_pairs(axis, step):
    pairs = []
    for x, y, z, c in places():
        to = [x, y, z]
        to[axis] = beside(to[axis], step, c)
        pairs.append((linear(x, y, z, c), linear(*to, c)))
    return pairs


CORE_PAIRS = [(linear(x, y, z, c), linear(x, y, z, 1 - c)) for x, y, z, c in places()]


def ring_order(place, core):
    first = beside(place, 0, core)
    return [place, beside(place, 1, core), first, beside(first, 1, core)]


def order_table():
    table = np.zeros((len(places()), 3, 8), np.int32)
    for x, y, z, c in places():
        here = linear(x, y, z, c)
        for half, core in enumerate((1 - c, c)):
            orders = [ring_order(p, core) for p in (x, y, z)]
            for slot, quarter in enumerate(orders[0]):
                step = half * 4 + slot
                table[here, 0, step] = core * 4 + quarter
                table[here, 1, step] = orders[1].index(quarter)
                table[here, 2, step] = orders[2].index(quarter)
    return table


def halves(value):
    high = value.astype(BF16)
    return high, (value - high.astype(F32)).astype(BF16)


def mul(a, b):
    return jnp.dot(a, b, preferred_element_type=F32)


def front_kernel(table, slab, sketch, sampled, gram, xs, ys, zs, xk, yk, zk, high, low, total, turned):
    step = pl.program_id(0)

    @pl.when(step < 8)
    def _():
        slab_high, slab_low = halves(slab[...])
        high[step] = slab_high
        low[step] = slab_low
        sketch_high, sketch_low = halves(sketch[...])
        both = mul(slab_high, jnp.concatenate([sketch_high, sketch_low], axis=1))
        part = both[:, :K] + (both[:, K:] + mul(slab_low, sketch_high))

        @pl.when(step == 0)
        def _():
            total[...] = part

        @pl.when(step > 0)
        def _():
            total[...] += part

    @pl.when(step == 7)
    def _():
        value = total[...]
        sampled[...] = value
        across = value.T
        product = jnp.dot(across, value, precision=HIGHEST, preferred_element_type=F32)
        gram[...] = jnp.concatenate([product[16 * t : 16 * t + 16] for t in range(8)], axis=1)
        across_high, across_low = halves(across)
        turned[...] = jnp.concatenate([across_high, across_low], axis=0)

    def products():
        chunk = table[0, step - 8]
        left = turned[...]
        both = mul(left, high[chunk])
        return both[:K] + (both[K:] + mul(left[:K], low[chunk]))

    @pl.when((step >= 8) & (step < 12))
    def _():
        value = products()
        for out, start, rows in zip((xs, ys, zs), STARTS, SPLIT):
            out[0] = value[start : start + rows]

    @pl.when(step >= 12)
    def _():
        value = products()
        for out, start, rows in zip((xk, yk, zk), STARTS, SPLIT):
            out[0] = value[start : start + rows]


def front(table, slab, sketch):
    rows = slab.shape[0]

    def sent(line):
        def index(i, t):
            at = jnp.clip(i - 8, 0, 3)
            return (at if line == 0 else t[line, at]), 0, 0

        return index

    def kept(line):
        def index(i, t):
            at = jnp.clip(i - 8, 4, 7)
            return (at - 4 if line == 0 else t[line, at]), 0, 0

        return index

    blocks = [pl.BlockSpec((1, SPLIT[a], CHUNK), sent(a)) for a in range(3)]
    blocks += [pl.BlockSpec((1, SPLIT[a], CHUNK), kept(a)) for a in range(3)]
    return pl.pallas_call(
        front_kernel,
        grid_spec=pltpu.PrefetchScalarGridSpec(
            num_scalar_prefetch=1,
            grid=(16,),
            in_specs=[
                pl.BlockSpec((rows, CHUNK), lambda i, t: (0, jnp.minimum(i, 7))),
                pl.BlockSpec((CHUNK, K), lambda i, t: (jnp.minimum(i, 7), 0)),
            ],
            out_specs=[
                pl.BlockSpec((rows, K), lambda i, t: (0, 0)),
                pl.BlockSpec((16, CHUNK), lambda i, t: (0, 0)),
                *blocks,
            ],
            scratch_shapes=[
                pltpu.VMEM((8, rows, CHUNK), BF16),
                pltpu.VMEM((8, rows, CHUNK), BF16),
                pltpu.VMEM((rows, K), F32),
                pltpu.VMEM((2 * K, rows), BF16),
            ],
        ),
        out_shape=[
            jax.ShapeDtypeStruct((rows, K), F32),
            jax.ShapeDtypeStruct((16, CHUNK), F32),
            *[jax.ShapeDtypeStruct((4, SPLIT[a % 3], CHUNK), F32) for a in range(6)],
        ],
        compiler_params=pltpu.CompilerParams(vmem_limit_bytes=36 * MIB),
        name="sample_and_product",
    )(table, slab, sketch)


def factor_kernel(scale, low_rows, high_rows, sampled, inverse, basis):
    folded = jnp.concatenate([low_rows[...], high_rows[...]], axis=0)
    left = jnp.concatenate([folded[:, K * t : K * t + K] for t in range(8)], axis=0)
    row = lax.broadcasted_iota(jnp.int32, (K, K), 0)
    col = lax.broadcasted_iota(jnp.int32, (K, K), 1)
    right = jnp.where(row == col, 1.0, 0.0).astype(F32)
    lefts = [left[8 * t : 8 * t + 8] for t in range(16)]
    rights = [right[8 * t : 8 * t + 8] for t in range(16)]
    sub = lax.broadcasted_iota(jnp.int32, (8, 1), 0)
    for j in range(K):
        tile, at = divmod(j, 8)
        pivot_row = lefts[tile][at : at + 1]
        down = 1.0 / pivot_row[:, j : j + 1]
        left_row = pivot_row * down
        right_row = rights[tile][at : at + 1] * down
        for t in range(tile, 16):
            factor = lefts[t][:, j : j + 1]
            if t == tile:
                factor = jnp.where(sub > at, factor, 0.0)
            lefts[t] = lefts[t] - factor * left_row
            rights[t] = rights[t] - factor * right_row
    left = jnp.concatenate(lefts, axis=0)
    right = jnp.concatenate(rights, axis=0)
    diagonal = jnp.sum(jnp.where(row == col, left, 0.0), axis=1, keepdims=True)
    value = right * lax.rsqrt(diagonal)
    inverse[...] = value
    basis[...] = scale * jnp.dot(sampled[...], value.T, precision=HIGHEST, preferred_element_type=F32)


def factor(low_rows, high_rows, sampled, scale):
    rows = sampled.shape[0]
    return pl.pallas_call(
        lambda *refs: factor_kernel(scale, *refs),
        out_shape=[jax.ShapeDtypeStruct((K, K), F32), jax.ShapeDtypeStruct((rows, K), F32)],
        cost_estimate=pl.CostEstimate(flops=8 * 10**9, bytes_accessed=MIB, transcendentals=0),
        compiler_params=pltpu.CompilerParams(vmem_limit_bytes=8 * MIB),
        name="factor_and_basis",
    )(low_rows, high_rows, sampled)


def apply_kernel(table, inverse, x, y, z, *rest):
    out = rest[-1]
    value = jnp.concatenate([x[0], y[0], z[0]], axis=0)
    out[...] = jnp.dot(inverse[...], value, precision=HIGHEST, preferred_element_type=F32)


def apply(table, inverse, parts, half, before=None):
    def slot(line):
        return lambda i, t: ((i if line == 0 else t[line, half * 4 + i]), 0, 0)

    in_specs = [pl.BlockSpec((K, K), lambda i, t: (0, 0))]
    in_specs += [pl.BlockSpec((1, SPLIT[a], CHUNK), slot(a)) for a in range(3)]
    args = [table, inverse, *parts]
    aliases = {}
    if before is not None:
        in_specs.append(pl.BlockSpec(memory_space=pl.ANY))
        args.append(before)
        aliases = {5: 0}
    return pl.pallas_call(
        apply_kernel,
        grid_spec=pltpu.PrefetchScalarGridSpec(
            num_scalar_prefetch=1,
            grid=(4,),
            in_specs=in_specs,
            out_specs=pl.BlockSpec((K, CHUNK), lambda i, t: (0, t[0, half * 4 + i])),
        ),
        out_shape=jax.ShapeDtypeStruct((K, 8 * CHUNK), F32),
        input_output_aliases=aliases,
        compiler_params=pltpu.CompilerParams(vmem_limit_bytes=12 * MIB),
        cost_estimate=pl.CostEstimate(flops=10**9, bytes_accessed=4 * MIB, transcendentals=0),
        name=f"apply_{half}",
    )(*args)


def send(value, pairs):
    return lax.ppermute(value, AXES, pairs)


def scatter_step(state, half, pairs):
    got = send(state[half:], pairs)
    return jnp.concatenate([state[:half], state[2 * half :]], axis=0) + got


def total_over_devices(kept, sent, extra):
    states = []
    for chain in range(3):
        rows = 4 * SPLIT[chain]
        own, other = kept[chain].reshape(rows, CHUNK), sent[chain].reshape(rows, CHUNK)
        if extra[chain] is not None:
            own = jnp.concatenate([own, extra[chain]], axis=0)
            other = jnp.concatenate([other, extra[chain]], axis=0)
        states.append(own + send(other, CORE_PAIRS))
    for step in range(2):
        for chain in range(3):
            half = SPLIT[chain] * (2 >> step)
            states[chain] = scatter_step(states[chain], half, ring_pairs(chain, step))
    for turn in (1, 2):
        for step in range(2):
            for chain in range(3):
                axis = (chain + turn) % 3
                states[chain] = states[chain] + send(states[chain], ring_pairs(axis, step))
    sums = [states[chain][SPLIT[chain] :] for chain in range(3)]
    parts = [states[chain][: SPLIT[chain]] for chain in range(3)]
    for step in (1, 0):
        for chain in range(3):
            got = send(parts[chain], ring_pairs(chain, step))
            parts[chain] = jnp.concatenate([parts[chain], got], axis=0)
    others = [send(part, CORE_PAIRS) for part in parts]

    def fold(arrays):
        return [a.reshape(4, SPLIT[chain], CHUNK) for chain, a in enumerate(arrays)]

    return fold(parts), fold(others), sums


def per_device(slab, sketch):
    total_rows = slab.shape[0] * lax.axis_size("row") * lax.axis_size("col")
    here = lax.axis_index("row") * lax.axis_size("col") + lax.axis_index("col")
    table = lax.dynamic_index_in_dim(jnp.asarray(order_table()), here, 0, keepdims=False)
    sampled, gram, *chunks = front(table, slab, sketch)
    own, other, sums = total_over_devices(chunks[3:], chunks[:3], (None, gram[:8], gram[8:]))
    inverse, basis = factor(sums[1], sums[2], sampled, math.sqrt(total_rows))
    projection = apply(table, inverse, own, 1)
    projection = apply(table, inverse, other, 0, projection)
    return basis, projection


def solution(mesh):
    return jax.shard_map(
        per_device,
        mesh=mesh,
        in_specs=(P(AXES, None), P()),
        out_specs=(P(AXES, None), P()),
        check_vma=False,
    )
```

```python
import math

import jax
import jax.numpy as jnp
from jax import lax
from jax.experimental import pallas as pl
from jax.experimental.pallas import tpu as pltpu
from jax.sharding import PartitionSpec as P

AXES = ("row", "col")
RING = 4
K = 128
CHUNK = 1024
HALF = 4096
WIDTH = (384, 384, 256)
STARTS = (0, 1536, 3072)
GRAM = 64
AHEAD = 8
QUARTERS = (156, 180)
SLOTS = (120, 180)
MIB = 2**20
F32 = jnp.float32
BF16 = jnp.bfloat16
HIGHEST = lax.Precision.HIGHEST
VMEM = pl.BlockSpec(memory_space=pltpu.VMEM)
HBM = pl.BlockSpec(memory_space=pltpu.HBM)


def places():
    return [
        (x, y, z, c) for y in range(RING) for c in range(2) for x in range(RING) for z in range(RING)
    ]


def linear(x, y, z, c):
    return (y * 2 + c) * RING * RING + x * RING + z


def side_of(x, y, z, core):
    return core ^ ((x + y + z) & 1)


def beside(place, step, side):
    return place ^ 1 if (step ^ side) == 0 else place ^ 3


def ring_pairs(axis, step):
    pairs = []
    for x, y, z, c in places():
        to = [x, y, z]
        to[axis] = beside(to[axis], step, side_of(x, y, z, c))
        pairs.append((linear(x, y, z, c), linear(*to, 1 - c)))
    return pairs


CORE_PAIRS = [(linear(x, y, z, c), linear(x, y, z, 1 - c)) for x, y, z, c in places()]


def here():
    row, col = lax.axis_index("row"), lax.axis_index("col")
    place = (col // RING, row // 2, col % RING)
    return place, side_of(*place, row % 2)


def two_bits(choices, side, at):
    return (jnp.where(side == 0, choices[0], choices[1]) >> (2 * at)) & 3


def halves(value):
    high = value.astype(BF16)
    return high, (value - high.astype(F32)).astype(BF16)


def mul(a, b):
    return jnp.dot(a, b, preferred_element_type=F32)


def products(left, high, low, outs, side):
    place, _ = here()
    for chain in range(3):
        width = WIDTH[chain]
        for pair in range(2):
            at = pl.ds(STARTS[chain] + 2 * pair * width, 2 * width)
            both = mul(left[...], high[:, at])
            value = both[:K] + (both[K:] + mul(left[:K], low[:, at]))
            for part in range(2):
                slot = two_bits(SLOTS, side, (2 * pair + part) ^ place[chain])
                rows = pl.ds(pl.multiple_of(slot * K, K), K)
                outs[chain][rows] = value[:, part * width : (part + 1) * width]


def sample_kernel(
    slab, sketch, sampled, left, high, low, xs, ys, zs,
    slab_here, sketch_here, sent_high, sent_low, slab_done, sketch_done,
):
    _, side = here()
    depth = slab_here.shape[0]

    def column(k):
        half = 1 - side if k < 4 else side
        return pl.multiple_of(half * HALF + (k % 4) * CHUNK, CHUNK)

    def slab_copy(k):
        return pltpu.make_async_copy(
            slab.at[:, pl.ds(column(k), CHUNK)], slab_here.at[k % depth], slab_done.at[k % depth]
        )

    def sketch_copy(k):
        return pltpu.make_async_copy(sketch.at[pl.ds(column(k), CHUNK)], sketch_here.at[k], sketch_done.at[k])

    for k in range(8):
        sketch_copy(k).start()
        if k < depth:
            slab_copy(k).start()
    for k in range(8):
        slab_copy(k).wait()
        slab_high, slab_low = halves(slab_here[k % depth])
        at = pl.ds((k % 4) * CHUNK, CHUNK)
        if k < 4:
            sent_high[:, at], sent_low[:, at] = slab_high, slab_low
        else:
            high[:, at], low[:, at] = slab_high, slab_low
        if k + depth < 8:
            slab_copy(k + depth).start()
        sketch_copy(k).wait()
        sketch_high, sketch_low = halves(sketch_here[k])
        both = mul(slab_high, jnp.concatenate([sketch_high, sketch_low], axis=1))
        value = both[:, :K] + (both[:, K:] + mul(slab_low, sketch_high))
        if k == 0:
            sampled[...] = value
        else:
            sampled[...] += value
    left[...] = jnp.concatenate(halves(sampled[...].T), axis=0)
    square = lax.dot_general(left[...], left[...], (((1,), (1,)), ((), ())), preferred_element_type=F32)
    gram = (square[:K, :K] + square[K:, K:]) + (square[:K, K:] + square[K:, :K])
    zs[4 * K :] = jnp.concatenate([gram[:GRAM], gram[GRAM:]], axis=1)
    products(left, sent_high, sent_low, (xs, ys, zs), 1 - side)


def sample(slab, sketch):
    rows = slab.shape[0]
    depth = 5
    return pl.pallas_call(
        sample_kernel,
        in_specs=[HBM, HBM],
        out_specs=[VMEM] * 7,
        out_shape=[
            jax.ShapeDtypeStruct((rows, K), F32),
            jax.ShapeDtypeStruct((2 * K, rows), BF16),
            jax.ShapeDtypeStruct((rows, HALF), BF16),
            jax.ShapeDtypeStruct((rows, HALF), BF16),
            jax.ShapeDtypeStruct((4 * K, WIDTH[0]), F32),
            jax.ShapeDtypeStruct((4 * K, WIDTH[1]), F32),
            jax.ShapeDtypeStruct((4 * K + GRAM, WIDTH[2]), F32),
        ],
        scratch_shapes=[
            pltpu.VMEM((depth, rows, CHUNK), F32),
            pltpu.VMEM((8, CHUNK, K), F32),
            pltpu.VMEM((rows, HALF), BF16),
            pltpu.VMEM((rows, HALF), BF16),
            pltpu.SemaphoreType.DMA((depth,)),
            pltpu.SemaphoreType.DMA((8,)),
        ],
        compiler_params=pltpu.CompilerParams(vmem_limit_bytes=40 * MIB),
        cost_estimate=pl.CostEstimate(flops=8 * 10**9, bytes_accessed=21 * MIB, transcendentals=0),
        name="sample",
    )(slab, sketch)


def keep_kernel(left, high, low, sent, x, y, z):
    _, side = here()
    z[4 * K :] = sent[4 * K :]
    products(left, high, low, (x, y, z), side)


def keep(left, high, low, sent):
    return pl.pallas_call(
        keep_kernel,
        in_specs=[VMEM] * 4,
        out_specs=[VMEM] * 3,
        out_shape=[
            jax.ShapeDtypeStruct((4 * K, WIDTH[0]), F32),
            jax.ShapeDtypeStruct((4 * K, WIDTH[1]), F32),
            jax.ShapeDtypeStruct((4 * K + GRAM, WIDTH[2]), F32),
        ],
        compiler_params=pltpu.CompilerParams(vmem_limit_bytes=20 * MIB),
        cost_estimate=pl.CostEstimate(flops=2 * 10**9, bytes_accessed=MIB, transcendentals=0),
        name="keep",
    )(left, high, low, sent)


def factor_kernel(folded, inverse):
    left = jnp.concatenate([folded[:, :K], folded[:, K:]], axis=0)
    row = lax.broadcasted_iota(jnp.int32, (K, K), 0)
    col = lax.broadcasted_iota(jnp.int32, (K, K), 1)
    right = jnp.where(row == col, 1.0, 0.0).astype(F32)
    lefts = [left[8 * t : 8 * t + 8] for t in range(16)]
    rights = [right[8 * t : 8 * t + 8] for t in range(16)]
    sub = lax.broadcasted_iota(jnp.int32, (8, K), 0)
    for start in range(0, K, AHEAD):
        tile, at = divmod(start, 8)
        columns = [
            [jnp.broadcast_to(lefts[t][:, start + k : start + k + 1], (8, K)) for t in range(tile, 16)]
            for k in range(AHEAD)
        ]
        rows_left = [jnp.broadcast_to(lefts[tile][at + k : at + k + 1], (8, K)) for k in range(AHEAD)]
        rows_right = [jnp.broadcast_to(rights[tile][at + k : at + k + 1], (8, K)) for k in range(AHEAD)]

        def entry(r, c):
            return jnp.broadcast_to(columns[c][0][at + r : at + r + 1], (8, K))

        for k in range(AHEAD):
            down = 1.0 / entry(k, k)
            below = [entry(m, k) for m in range(k + 1, AHEAD)]
            rows_left[k] = rows_left[k] * down
            rows_right[k] = rows_right[k] * down
            for m in range(k + 1, AHEAD):
                rows_left[m] = rows_left[m] - below[m - k - 1] * rows_left[k]
                rows_right[m] = rows_right[m] - below[m - k - 1] * rows_right[k]
                share = below[m - k - 1] * down
                columns[m] = [own - other * share for own, other in zip(columns[m], columns[k])]
        for k in range(AHEAD):
            columns[k][0] = jnp.where(sub > at + k, columns[k][0], 0.0)
        for t in range(tile, 16):
            for k in range(AHEAD):
                lefts[t] = lefts[t] - columns[k][t - tile] * rows_left[k]
                rights[t] = rights[t] - columns[k][t - tile] * rows_right[k]
    left = jnp.concatenate(lefts, axis=0)
    right = jnp.concatenate(rights, axis=0)
    diagonal = jnp.sum(jnp.where(row == col, left, 0.0), axis=1, keepdims=True)
    inverse[...] = right * lax.rsqrt(diagonal)


def factor(folded):
    return pl.pallas_call(
        factor_kernel,
        in_specs=[VMEM],
        out_specs=VMEM,
        out_shape=jax.ShapeDtypeStruct((K, K), F32),
        cost_estimate=pl.CostEstimate(flops=6 * 10**9, bytes_accessed=MIB, transcendentals=0),
        compiler_params=pltpu.CompilerParams(vmem_limit_bytes=8 * MIB),
        name="factor",
    )(folded)


def basis_kernel(scale, inverse, sampled, out):
    out[...] = scale * jnp.dot(sampled[...], inverse[...].T, precision=HIGHEST, preferred_element_type=F32)


def basis(inverse, sampled, scale):
    return pl.pallas_call(
        lambda *refs: basis_kernel(scale, *refs),
        in_specs=[VMEM, VMEM],
        out_specs=VMEM,
        out_shape=jax.ShapeDtypeStruct(sampled.shape, F32),
        cost_estimate=pl.CostEstimate(flops=10**9, bytes_accessed=MIB, transcendentals=0),
        compiler_params=pltpu.CompilerParams(vmem_limit_bytes=8 * MIB),
        name="basis",
    )(inverse, sampled)


def call_in_turn(body, args, shapes, after, name):
    extra = [] if after is None else [after]
    any_space = pl.BlockSpec(memory_space=pl.ANY)

    def kernel(*refs):
        body(*refs[: len(args)], *refs[len(args) + len(extra) :])

    return pl.pallas_call(
        kernel,
        in_specs=[VMEM] * len(args) + [any_space] * len(extra),
        out_specs=[VMEM] * len(shapes),
        out_shape=[jax.ShapeDtypeStruct(shape, F32) for shape in shapes],
        compiler_params=pltpu.CompilerParams(vmem_limit_bytes=MIB),
        cost_estimate=pl.CostEstimate(flops=10**8, bytes_accessed=MIB // 4, transcendentals=0),
        name=name,
    )(*args, *extra)


def split(total, rest, keep, hand):
    half = keep.shape[0]
    keep[...] = total[:half]
    hand[:half] = total[half:]
    if rest is not None:
        hand[half:] = rest


def sum_cores(kept, got, after):
    rows, width = kept.shape

    def body(kept_ref, got_ref, keep, hand):
        rest = kept_ref[4 * K :] + got_ref[4 * K :] if rows > 4 * K else None
        split(kept_ref[: 4 * K] + got_ref[: 4 * K], rest, keep, hand)

    return call_in_turn(body, [kept, got], [(2 * K, width), (rows - 2 * K, width)], after, "sum_cores")


def sum_half(kept, handed, got, after):
    half, width = kept.shape
    rest = handed.shape[0] - half

    def total(kept_ref, handed_ref, got_ref):
        more = handed_ref[half:] + got_ref[half:] if rest else None
        return kept_ref[...] + got_ref[:half], more

    def halve(kept_ref, handed_ref, got_ref, keep, hand):
        split(*total(kept_ref, handed_ref, got_ref), keep, hand)

    def finish(kept_ref, handed_ref, got_ref, out):
        value, more = total(kept_ref, handed_ref, got_ref)
        out[:half] = value
        if rest:
            out[half:] = more

    args = [kept, handed, got]
    if half == K:
        return call_in_turn(finish, args, [(half + rest, width)], after, "sum_quarter")[0]
    return call_in_turn(halve, args, [(half // 2, width), (half // 2 + rest, width)], after, "sum_half")


def sum_whole(state, got, after):
    def body(state_ref, got_ref, out):
        out[...] = state_ref[...] + got_ref[...]

    return call_in_turn(body, [state, got], [state.shape], after, "sum_whole")[0]


def sum_last(state, got, after):
    rows, width = state.shape

    def body(state_ref, got_ref, own, *rest):
        own[...] = state_ref[:K] + got_ref[:K]
        if rest:
            rest[0][...] = state_ref[K:] + got_ref[K:]

    shapes = [(K, width)] + ([(rows - K, width)] if rows > K else [])
    return call_in_turn(body, [state, got], shapes, after, "sum_last")


def join(own, got, after):
    rows, width = own.shape

    def body(own_ref, got_ref, out):
        out[:rows] = own_ref[...]
        out[rows:] = got_ref[...]

    return call_in_turn(body, [own, got], [(2 * rows, width)], after, "join")[0]


def pass_on(value, after):
    any_space = pl.BlockSpec(memory_space=pl.ANY)
    return pl.pallas_call(
        lambda *refs: None,
        in_specs=[any_space] * 2,
        out_specs=any_space,
        out_shape=jax.ShapeDtypeStruct(value.shape, value.dtype),
        input_output_aliases={0: 0},
        compiler_params=pltpu.CompilerParams(vmem_limit_bytes=MIB),
        name="pass_on",
    )(value, after)


def apply_kernel(pieces, inverse, *rest):
    arrays, (out, *ready, done) = rest[: len(pieces)], rest[-5:]
    place, side = here()
    high, low = halves(inverse[...])
    wide = jnp.concatenate([high, high], axis=1)
    copies = []
    filled = [0, 0, 0]
    for array, (chain, other, first) in zip(arrays, pieces):
        owner = 1 - side if other else side
        width = WIDTH[chain]
        for i in range(2):
            value_high, value_low = halves(array[K * i : K * i + K])
            at = filled[chain]
            filled[chain] += 1
            stacked = jnp.concatenate([value_high, value_low], axis=0)
            ready[chain][at] = mul(wide, stacked) + mul(low, value_high)
            quarter = place[chain] ^ two_bits(QUARTERS, owner, first + i)
            column = pl.multiple_of(owner * HALF + STARTS[chain] + quarter * width, K)
            copies.append(
                pltpu.make_async_copy(ready[chain].at[at], out.at[:, pl.ds(column, width)], done.at[len(copies)])
            )
            copies[-1].start()
    for copy in copies:
        copy.wait()


def apply(inverse, parts, pieces, before, name):
    aliases = {} if before is None else {1 + len(parts): 0}
    args = [inverse, *parts] + ([] if before is None else [before])
    most = [2 * sum(piece[0] == chain for piece in pieces) for chain in range(3)]
    return pl.pallas_call(
        lambda *refs: apply_kernel(pieces, *refs),
        in_specs=[VMEM] * (1 + len(parts)) + [HBM] * len(aliases),
        out_specs=HBM,
        out_shape=jax.ShapeDtypeStruct((K, 2 * HALF), F32),
        scratch_shapes=[
            *[pltpu.VMEM((max(most[chain], 1), K, WIDTH[chain]), F32) for chain in range(3)],
            pltpu.SemaphoreType.DMA((2 * len(pieces),)),
        ],
        input_output_aliases=aliases,
        compiler_params=pltpu.CompilerParams(vmem_limit_bytes=12 * MIB),
        cost_estimate=pl.CostEstimate(flops=10**9, bytes_accessed=2 * MIB, transcendentals=0),
        name=name,
    )(*args)


def send(value, pairs):
    return lax.ppermute(value, AXES, pairs)


def per_device(slab, sketch):
    total_rows = slab.shape[0] * lax.axis_size("row") * lax.axis_size("col")
    turns = (0, 1, 2)
    sampled, left, high, low, *sent = sample(slab, sketch)
    kept = keep(left, high, low, sent[2])
    after = None
    kept, handed, states, near, far = list(kept), [None] * 3, [None] * 3, [None] * 3, [None] * 3
    for chain in turns:
        got = send(sent[chain], CORE_PAIRS)
        kept[chain], handed[chain] = sum_cores(kept[chain], got, after)
        after = kept[chain]
    for chain in turns:
        got = send(handed[chain], ring_pairs(chain, 0))
        kept[chain], handed[chain] = sum_half(kept[chain], handed[chain], got, after)
        after = kept[chain]
    for chain in turns:
        got = send(handed[chain], ring_pairs(chain, 1))
        states[chain] = after = sum_half(kept[chain], handed[chain], got, after)
    for turn, step in ((1, 0), (1, 1), (2, 0)):
        for chain in turns:
            got = send(states[chain], ring_pairs((chain + turn) % 3, step))
            states[chain] = after = sum_whole(states[chain], got, after)
    gram = None
    for chain in turns:
        got = send(states[chain], ring_pairs((chain + 2) % 3, 1))
        states[chain], *rest = sum_last(states[chain], got, after)
        after = states[chain]
        gram = rest[0] if rest else gram
    for chain in turns:
        near[chain] = after = join(states[chain], send(states[chain], ring_pairs(chain, 1)), after)
    inverse = factor(pass_on(gram, after))
    for chain in turns:
        far[chain] = pass_on(send(near[chain], ring_pairs(chain, 0)), inverse)
    near_other = [send(pass_on(part, later), CORE_PAIRS) for part, later in zip(near, far)]
    far_other = [send(part, CORE_PAIRS) for part in far]
    out = apply(inverse, near + far, [(a, 0, first) for first in (0, 2) for a in range(3)], None, "apply_own")
    out = apply(inverse, near_other, [(a, 1, 0) for a in range(3)], out, "apply_near")
    out = apply(inverse, far_other, [(a, 1, 2) for a in range(3)], out, "apply_far")
    return basis(inverse, sampled, math.sqrt(total_rows)), out


def solution(mesh):
    return jax.shard_map(
        per_device,
        mesh=mesh,
        in_specs=(P(AXES, None), P()),
        out_specs=(P(AXES, None), P()),
        check_vma=False,
    )
```

```python
import math

import jax
import jax.numpy as jnp
from jax import lax
from jax.experimental import pallas as pl
from jax.experimental.pallas import tpu as pltpu
from jax.sharding import PartitionSpec as P

AXES = ("row", "col")
RING = 4
K = 128
CHUNK = 1024
HALF = 4096
WIDTH = (384, 384, 256)
STARTS = (0, 1536, 3072)
GRAM = 64
FLIP = (0, 1, 0)
AHEAD = 8
QUARTERS = (156, 180)
SLOTS = (120, 180)
MIB = 2**20
F32 = jnp.float32
BF16 = jnp.bfloat16
HIGHEST = lax.Precision.HIGHEST
VMEM = pl.BlockSpec(memory_space=pltpu.VMEM)
HBM = pl.BlockSpec(memory_space=pltpu.HBM)


def places():
    return [
        (x, y, z, c) for y in range(RING) for c in range(2) for x in range(RING) for z in range(RING)
    ]


def linear(x, y, z, c):
    return (y * 2 + c) * RING * RING + x * RING + z


def side_of(x, y, z, core):
    return core ^ ((x + y + z) & 1)


def beside(place, step, side):
    return place ^ 1 if (step ^ side) == 0 else place ^ 3


def ring_pairs(axis, step, flip=0):
    pairs = []
    for x, y, z, c in places():
        to = [x, y, z]
        to[axis] = beside(to[axis], step ^ flip, side_of(x, y, z, c))
        pairs.append((linear(x, y, z, c), linear(*to, 1 - c)))
    return pairs


CORE_PAIRS = [(linear(x, y, z, c), linear(x, y, z, 1 - c)) for x, y, z, c in places()]


def here():
    row, col = lax.axis_index("row"), lax.axis_index("col")
    place = (col // RING, row // 2, col % RING)
    return place, side_of(*place, row % 2)


def two_bits(choices, side, at):
    return (jnp.where(side == 0, choices[0], choices[1]) >> (2 * at)) & 3


def halves(value):
    high = value.astype(BF16)
    return high, (value - high.astype(F32)).astype(BF16)


def mul(a, b):
    return jnp.dot(a, b, preferred_element_type=F32)


def product(chain, side, left, high, low, out):
    place, _ = here()
    width = WIDTH[chain]
    for i in range(4):
        first = max(STARTS[chain], i * CHUNK)
        last = min(STARTS[chain] + 4 * width, (i + 1) * CHUNK)
        if first >= last:
            continue
        at = slice(first - i * CHUNK, last - i * CHUNK)
        both = mul(left[...], high[i, :, at])
        value = both[:K] + (both[K:] + mul(left[:K], low[i, :, at]))
        begin = first
        while begin < last:
            quarter, within = divmod(begin - STARTS[chain], width)
            size = min(width - within, last - begin)
            slot = two_bits(SLOTS, side ^ FLIP[chain], quarter ^ place[chain])
            rows = pl.ds(pl.multiple_of(slot * K, K), K)
            out[rows, within : within + size] = value[:, begin - first : begin - first + size]
            begin += size


def sample_kernel(
    slab, sketch, sampled, left, sent_high, sent_low, high, low, xs,
    slab_here, sketch_here, slab_done, sketch_done,
):
    _, side = here()
    depth = slab_here.shape[0]

    def column(k):
        half = 1 - side if k < 4 else side
        return pl.multiple_of(half * HALF + (k % 4) * CHUNK, CHUNK)

    def slab_copy(k):
        return pltpu.make_async_copy(
            slab.at[:, pl.ds(column(k), CHUNK)], slab_here.at[k % depth], slab_done.at[k % depth]
        )

    def sketch_copy(k):
        return pltpu.make_async_copy(sketch.at[pl.ds(column(k), CHUNK)], sketch_here.at[k], sketch_done.at[k])

    for k in range(8):
        sketch_copy(k).start()
        if k < depth:
            slab_copy(k).start()
    for k in range(8):
        slab_copy(k).wait()
        sketch_copy(k).wait()
        slab_high, slab_low = halves(slab_here[k % depth])
        if k < 4:
            sent_high[k], sent_low[k] = slab_high, slab_low
        else:
            high[k - 4], low[k - 4] = slab_high, slab_low
        sketch_high, sketch_low = halves(sketch_here[k])
        both = mul(slab_high, jnp.concatenate([sketch_high, sketch_low], axis=1))
        value = both[:, :K] + (both[:, K:] + mul(slab_low, sketch_high))
        if k == 0:
            sampled[...] = value
        else:
            sampled[...] += value
        if k + depth < 8:
            slab_copy(k + depth).start()
    left[...] = jnp.concatenate(halves(sampled[...].T), axis=0)
    product(0, 1 - side, left, sent_high, sent_low, xs)


def sample(slab, sketch):
    rows = slab.shape[0]
    depth = 5
    return pl.pallas_call(
        sample_kernel,
        in_specs=[HBM, HBM],
        out_specs=[VMEM] * 7,
        out_shape=[
            jax.ShapeDtypeStruct((rows, K), F32),
            jax.ShapeDtypeStruct((2 * K, rows), BF16),
            *[jax.ShapeDtypeStruct((4, rows, CHUNK), BF16)] * 4,
            jax.ShapeDtypeStruct((4 * K, WIDTH[0]), F32),
        ],
        scratch_shapes=[
            pltpu.VMEM((depth, rows, CHUNK), F32),
            pltpu.VMEM((8, CHUNK, K), F32),
            pltpu.SemaphoreType.DMA((depth,)),
            pltpu.SemaphoreType.DMA((8,)),
        ],
        compiler_params=pltpu.CompilerParams(vmem_limit_bytes=34 * MIB),
        cost_estimate=pl.CostEstimate(flops=8 * 10**9, bytes_accessed=21 * MIB, transcendentals=0),
        name="sample",
    )(slab, sketch)


def rest_kernel(left, high, low, after, y, z):
    _, side = here()
    product(1, 1 - side, left, high, low, y)
    square = lax.dot_general(left[...], left[...], (((1,), (1,)), ((), ())), preferred_element_type=F32)
    gram = (square[:K, :K] + square[K:, K:]) + (square[:K, K:] + square[K:, :K])
    z[4 * K :] = jnp.concatenate([gram[:GRAM], gram[GRAM:]], axis=1)
    product(2, 1 - side, left, high, low, z)


def rest_to_send(left, high, low, after):
    return pl.pallas_call(
        rest_kernel,
        in_specs=[VMEM] * 3 + [pl.BlockSpec(memory_space=pl.ANY)],
        out_specs=[VMEM] * 2,
        out_shape=[
            jax.ShapeDtypeStruct((4 * K, WIDTH[1]), F32),
            jax.ShapeDtypeStruct((4 * K + GRAM, WIDTH[2]), F32),
        ],
        compiler_params=pltpu.CompilerParams(vmem_limit_bytes=20 * MIB),
        cost_estimate=pl.CostEstimate(flops=15 * 10**8, bytes_accessed=MIB, transcendentals=0),
        name="rest_to_send",
    )(left, high, low, after)


def keep_kernel(chain, left, high, low, *rest):
    _, side = here()
    out = rest[-1]
    if len(rest) > 2:
        out[4 * K :] = rest[0][4 * K :]
    product(chain, side, left, high, low, out)


def keep(chain, left, high, low, sent, after):
    rows, width = sent.shape
    args = [left, high, low] + ([sent] if rows > 4 * K else []) + [after]
    return pl.pallas_call(
        lambda *refs: keep_kernel(chain, *refs),
        in_specs=[VMEM] * (len(args) - 1) + [pl.BlockSpec(memory_space=pl.ANY)],
        out_specs=VMEM,
        out_shape=jax.ShapeDtypeStruct((rows, width), F32),
        compiler_params=pltpu.CompilerParams(vmem_limit_bytes=20 * MIB),
        cost_estimate=pl.CostEstimate(flops=7 * 10**8, bytes_accessed=MIB, transcendentals=0),
        name="keep",
    )(*args)


def factor_kernel(folded, inverse):
    left = jnp.concatenate([folded[:, :K], folded[:, K:]], axis=0)
    row = lax.broadcasted_iota(jnp.int32, (K, K), 0)
    col = lax.broadcasted_iota(jnp.int32, (K, K), 1)
    right = jnp.where(row == col, 1.0, 0.0).astype(F32)
    lefts = [left[8 * t : 8 * t + 8] for t in range(16)]
    rights = [right[8 * t : 8 * t + 8] for t in range(16)]
    sub = lax.broadcasted_iota(jnp.int32, (8, K), 0)
    for start in range(0, K, AHEAD):
        tile, at = divmod(start, 8)
        columns = [
            [jnp.broadcast_to(lefts[t][:, start + k : start + k + 1], (8, K)) for t in range(tile, 16)]
            for k in range(AHEAD)
        ]
        rows_left = [jnp.broadcast_to(lefts[tile][at + k : at + k + 1], (8, K)) for k in range(AHEAD)]
        rows_right = [jnp.broadcast_to(rights[tile][at + k : at + k + 1], (8, K)) for k in range(AHEAD)]

        def entry(r, c):
            return jnp.broadcast_to(columns[c][0][at + r : at + r + 1], (8, K))

        for k in range(AHEAD):
            down = 1.0 / entry(k, k)
            below = [entry(m, k) for m in range(k + 1, AHEAD)]
            rows_left[k] = rows_left[k] * down
            rows_right[k] = rows_right[k] * down
            for m in range(k + 1, AHEAD):
                rows_left[m] = rows_left[m] - below[m - k - 1] * rows_left[k]
                rows_right[m] = rows_right[m] - below[m - k - 1] * rows_right[k]
                share = below[m - k - 1] * down
                columns[m] = [own - other * share for own, other in zip(columns[m], columns[k])]
        for k in range(AHEAD):
            columns[k][0] = jnp.where(sub > at + k, columns[k][0], 0.0)
        for t in range(tile, 16):
            for k in range(AHEAD):
                lefts[t] = lefts[t] - columns[k][t - tile] * rows_left[k]
                rights[t] = rights[t] - columns[k][t - tile] * rows_right[k]
    left = jnp.concatenate(lefts, axis=0)
    right = jnp.concatenate(rights, axis=0)
    diagonal = jnp.sum(jnp.where(row == col, left, 0.0), axis=1, keepdims=True)
    inverse[...] = right * lax.rsqrt(diagonal)


def factor(folded):
    return pl.pallas_call(
        factor_kernel,
        in_specs=[VMEM],
        out_specs=VMEM,
        out_shape=jax.ShapeDtypeStruct((K, K), F32),
        cost_estimate=pl.CostEstimate(flops=6 * 10**9, bytes_accessed=MIB, transcendentals=0),
        compiler_params=pltpu.CompilerParams(vmem_limit_bytes=8 * MIB),
        name="factor",
    )(folded)


def call_in_turn(body, args, shapes, after, name):
    extra = [] if after is None else [after]
    any_space = pl.BlockSpec(memory_space=pl.ANY)

    def kernel(*refs):
        body(*refs[: len(args)], *refs[len(args) + len(extra) :])

    return pl.pallas_call(
        kernel,
        in_specs=[VMEM] * len(args) + [any_space] * len(extra),
        out_specs=[VMEM] * len(shapes),
        out_shape=[jax.ShapeDtypeStruct(shape, F32) for shape in shapes],
        compiler_params=pltpu.CompilerParams(vmem_limit_bytes=MIB),
        cost_estimate=pl.CostEstimate(flops=10**8, bytes_accessed=MIB // 4, transcendentals=0),
        name=name,
    )(*args, *extra)


def split(total, rest, keep, hand):
    half = keep.shape[0]
    keep[...] = total[:half]
    hand[:half] = total[half:]
    if rest is not None:
        hand[half:] = rest


def sum_cores(kept, got, after):
    rows, width = kept.shape

    def body(kept_ref, got_ref, keep, hand):
        rest = kept_ref[4 * K :] + got_ref[4 * K :] if rows > 4 * K else None
        split(kept_ref[: 4 * K] + got_ref[: 4 * K], rest, keep, hand)

    return call_in_turn(body, [kept, got], [(2 * K, width), (rows - 2 * K, width)], after, "sum_cores")


def sum_half(kept, handed, got, after):
    half, width = kept.shape
    rest = handed.shape[0] - half

    def total(kept_ref, handed_ref, got_ref):
        more = handed_ref[half:] + got_ref[half:] if rest else None
        return kept_ref[...] + got_ref[:half], more

    def halve(kept_ref, handed_ref, got_ref, keep, hand):
        split(*total(kept_ref, handed_ref, got_ref), keep, hand)

    def finish(kept_ref, handed_ref, got_ref, out):
        value, more = total(kept_ref, handed_ref, got_ref)
        out[:half] = value
        if rest:
            out[half:] = more

    args = [kept, handed, got]
    if half == K:
        return call_in_turn(finish, args, [(half + rest, width)], after, "sum_quarter")[0]
    return call_in_turn(halve, args, [(half // 2, width), (half // 2 + rest, width)], after, "sum_half")


def sum_whole(state, got, after):
    def body(state_ref, got_ref, out):
        out[...] = state_ref[...] + got_ref[...]

    return call_in_turn(body, [state, got], [state.shape], after, "sum_whole")[0]


def sum_last(state, got, after):
    rows, width = state.shape

    def body(state_ref, got_ref, own, *rest):
        own[...] = state_ref[:K] + got_ref[:K]
        if rest:
            rest[0][...] = state_ref[K:] + got_ref[K:]

    shapes = [(K, width)] + ([(rows - K, width)] if rows > K else [])
    return call_in_turn(body, [state, got], shapes, after, "sum_last")


def join(own, got, after):
    rows, width = own.shape

    def body(own_ref, got_ref, out):
        out[:rows] = own_ref[...]
        out[rows:] = got_ref[...]

    return call_in_turn(body, [own, got], [(2 * rows, width)], after, "join")[0]


def pass_on(value, after):
    any_space = pl.BlockSpec(memory_space=pl.ANY)
    return pl.pallas_call(
        lambda *refs: None,
        in_specs=[any_space] * 2,
        out_specs=any_space,
        out_shape=jax.ShapeDtypeStruct(value.shape, value.dtype),
        input_output_aliases={0: 0},
        compiler_params=pltpu.CompilerParams(vmem_limit_bytes=MIB),
        name="pass_on",
    )(value, after)


def put_products(pieces, arrays, inverse, out, ready, done):
    place, side = here()
    high, low = halves(inverse[...])
    wide = jnp.concatenate([high, high], axis=1)
    copies = []
    filled = [0, 0, 0]
    for array, (chain, other, first) in zip(arrays, pieces):
        owner = 1 - side if other else side
        width = WIDTH[chain]
        for i in range(2):
            value_high, value_low = halves(array[K * i : K * i + K])
            at = filled[chain]
            filled[chain] += 1
            stacked = jnp.concatenate([value_high, value_low], axis=0)
            ready[chain][at] = mul(wide, stacked) + mul(low, value_high)
            quarter = place[chain] ^ two_bits(QUARTERS, owner ^ FLIP[chain], first + i)
            column = pl.multiple_of(owner * HALF + STARTS[chain] + quarter * width, K)
            copies.append(
                pltpu.make_async_copy(ready[chain].at[at], out.at[:, pl.ds(column, width)], done.at[len(copies)])
            )
            copies[-1].start()
    return copies


def apply_first_kernel(pieces, scale, inverse, sampled, *rest):
    arrays, (out, basis, mark, *ready, basis_ready, done, basis_done) = rest[: len(pieces)], rest[len(pieces) :]
    mark[...] = jnp.zeros_like(mark)
    copies = put_products(pieces, arrays, inverse, out, ready, done)
    across_high, across_low = halves(inverse[...].T)
    high, low = halves(sampled[...])
    wide = jnp.concatenate([across_high, across_high], axis=0)
    basis_ready[...] = scale * (mul(jnp.concatenate([high, low], axis=1), wide) + mul(high, across_low))
    copies.append(pltpu.make_async_copy(basis_ready, basis, basis_done))
    copies[-1].start()
    for copy in copies:
        copy.wait()


def apply_next_kernel(pieces, inverse, *rest):
    arrays, (_, out, *ready, done) = rest[: len(pieces)], rest[len(pieces) :]
    for copy in put_products(pieces, arrays, inverse, out, ready, done):
        copy.wait()


def apply_scratch(pieces):
    most = [2 * sum(piece[0] == chain for piece in pieces) for chain in range(3)]
    return [pltpu.VMEM((most[chain], K, WIDTH[chain]), F32) for chain in range(3)]


def apply_first(inverse, parts, pieces, sampled, scale):
    return pl.pallas_call(
        lambda *refs: apply_first_kernel(pieces, scale, *refs),
        in_specs=[VMEM] * (2 + len(parts)),
        out_specs=[HBM, HBM, VMEM],
        out_shape=[
            jax.ShapeDtypeStruct((K, 2 * HALF), F32),
            jax.ShapeDtypeStruct(sampled.shape, F32),
            jax.ShapeDtypeStruct((8, K), F32),
        ],
        scratch_shapes=[
            *apply_scratch(pieces),
            pltpu.VMEM(sampled.shape, F32),
            pltpu.SemaphoreType.DMA((2 * len(pieces),)),
            pltpu.SemaphoreType.DMA,
        ],
        compiler_params=pltpu.CompilerParams(vmem_limit_bytes=12 * MIB),
        cost_estimate=pl.CostEstimate(flops=10**9, bytes_accessed=2 * MIB, transcendentals=0),
        name="apply_first",
    )(inverse, sampled, *parts)


def apply_next(inverse, parts, pieces, before):
    return pl.pallas_call(
        lambda *refs: apply_next_kernel(pieces, *refs),
        in_specs=[VMEM] * (1 + len(parts)) + [HBM],
        out_specs=HBM,
        out_shape=jax.ShapeDtypeStruct((K, 2 * HALF), F32),
        scratch_shapes=[*apply_scratch(pieces), pltpu.SemaphoreType.DMA((2 * len(pieces),))],
        input_output_aliases={1 + len(parts): 0},
        compiler_params=pltpu.CompilerParams(vmem_limit_bytes=12 * MIB),
        cost_estimate=pl.CostEstimate(flops=10**9, bytes_accessed=2 * MIB, transcendentals=0),
        name="apply_next",
    )(inverse, *parts, before)


def send(value, pairs):
    return lax.ppermute(value, AXES, pairs)


def per_device(slab, sketch):
    total_rows = slab.shape[0] * lax.axis_size("row") * lax.axis_size("col")
    turns = (0, 1, 2)
    sampled, left, sent_high, sent_low, high, low, first = sample(slab, sketch)
    sent = [first, *rest_to_send(left, sent_high, sent_low, first)]
    after = sent[2]
    kept, handed, states, near, far = [None] * 3, [None] * 3, [None] * 3, [None] * 3, [None] * 3
    for chain in turns:
        got = send(sent[chain], CORE_PAIRS)
        own = keep(chain, left, high, low, sent[chain], after)
        kept[chain], handed[chain] = sum_cores(own, got, None)
        after = kept[chain]
    for chain in turns:
        got = send(handed[chain], ring_pairs(chain, 0, FLIP[chain]))
        kept[chain], handed[chain] = sum_half(kept[chain], handed[chain], got, after)
        after = kept[chain]
    for chain in turns:
        got = send(handed[chain], ring_pairs(chain, 1, FLIP[chain]))
        states[chain] = after = sum_half(kept[chain], handed[chain], got, after)
    for turn, step in ((1, 0), (1, 1), (2, 0)):
        for chain in turns:
            got = send(states[chain], ring_pairs((chain + turn) % 3, step, FLIP[chain]))
            states[chain] = after = sum_whole(states[chain], got, after)
    gram = None
    for chain in turns:
        got = send(states[chain], ring_pairs((chain + 2) % 3, 1, FLIP[chain]))
        states[chain], *rest = sum_last(states[chain], got, after)
        after = states[chain]
        gram = rest[0] if rest else gram
    for chain in turns:
        near[chain] = after = join(states[chain], send(states[chain], ring_pairs(chain, 1, FLIP[chain])), after)
    inverse = factor(pass_on(gram, after))
    scale = math.sqrt(total_rows)
    out, basis, mark = apply_first(inverse, near, [(a, 0, 0) for a in range(3)], sampled, scale)
    for chain in turns:
        far[chain] = pass_on(send(near[chain], ring_pairs(chain, 0, FLIP[chain])), mark)
    near_other = [send(pass_on(part, later), CORE_PAIRS) for part, later in zip(near, far)]
    far_other = [send(part, CORE_PAIRS) for part in far]
    middle = [(a, 0, 2) for a in range(3)] + [(a, 1, 0) for a in range(3)]
    out = apply_next(inverse, far + near_other, middle, out)
    out = apply_next(inverse, far_other, [(a, 1, 2) for a in range(3)], out)
    return basis, out


def solution(mesh):
    return jax.shard_map(
        per_device,
        mesh=mesh,
        in_specs=(P(AXES, None), P()),
        out_specs=(P(AXES, None), P()),
        check_vma=False,
    )
```

```python
import math

import jax
import jax.numpy as jnp
from jax import lax
from jax.experimental import pallas as pl
from jax.experimental.pallas import tpu as pltpu
from jax.sharding import PartitionSpec as P

AXES = ("row", "col")
RING = 4
K = 128
CHUNK = 1024
HALF = 4096
WIDTH = (384, 384, 256)
STARTS = (0, 1536, 3072)
GRAM = 64
FLIP = (0, 1, 0)
AHEAD = 8
QUARTERS = (156, 180)
SLOTS = (120, 180)
MIB = 2**20
F32 = jnp.float32
BF16 = jnp.bfloat16
HIGHEST = lax.Precision.HIGHEST
VMEM = pl.BlockSpec(memory_space=pltpu.VMEM)
HBM = pl.BlockSpec(memory_space=pltpu.HBM)


def places():
    return [
        (x, y, z, c) for y in range(RING) for c in range(2) for x in range(RING) for z in range(RING)
    ]


def linear(x, y, z, c):
    return (y * 2 + c) * RING * RING + x * RING + z


def side_of(x, y, z, core):
    return core ^ ((x + y + z) & 1)


def beside(place, step, side):
    return place ^ 1 if (step ^ side) == 0 else place ^ 3


def ring_pairs(axis, step, flip=0):
    pairs = []
    for x, y, z, c in places():
        to = [x, y, z]
        to[axis] = beside(to[axis], step ^ flip, side_of(x, y, z, c))
        pairs.append((linear(x, y, z, c), linear(*to, 1 - c)))
    return pairs


CORE_PAIRS = [(linear(x, y, z, c), linear(x, y, z, 1 - c)) for x, y, z, c in places()]


def here():
    row, col = lax.axis_index("row"), lax.axis_index("col")
    place = (col // RING, row // 2, col % RING)
    return place, side_of(*place, row % 2)


def two_bits(choices, side, at):
    return (jnp.where(side == 0, choices[0], choices[1]) >> (2 * at)) & 3


def halves(value):
    high = value.astype(BF16)
    return high, (value - high.astype(F32)).astype(BF16)


def mul(a, b):
    return jnp.dot(a, b, preferred_element_type=F32)


def product(chain, side, left, high, low, out):
    place, _ = here()
    width = WIDTH[chain]
    for i in range(4):
        first = max(STARTS[chain], i * CHUNK)
        last = min(STARTS[chain] + 4 * width, (i + 1) * CHUNK)
        if first >= last:
            continue
        at = slice(first - i * CHUNK, last - i * CHUNK)
        both = mul(left[...], high[i, :, at])
        value = both[:K] + (both[K:] + mul(left[:K], low[i, :, at]))
        begin = first
        while begin < last:
            quarter, within = divmod(begin - STARTS[chain], width)
            size = min(width - within, last - begin)
            slot = two_bits(SLOTS, side ^ FLIP[chain], quarter ^ place[chain])
            rows = pl.ds(pl.multiple_of(slot * K, K), K)
            out[rows, within : within + size] = value[:, begin - first : begin - first + size]
            begin += size


def sample_kernel(
    slab, sketch, sampled, left, sent_high, sent_low, high, low, xs,
    slab_here, sketch_here, slab_done, sketch_done,
):
    _, side = here()
    depth = slab_here.shape[0]

    def column(k):
        half = 1 - side if k < 4 else side
        return pl.multiple_of(half * HALF + (k % 4) * CHUNK, CHUNK)

    def slab_copy(k):
        return pltpu.make_async_copy(
            slab.at[:, pl.ds(column(k), CHUNK)], slab_here.at[k % depth], slab_done.at[k % depth]
        )

    def sketch_copy(k):
        return pltpu.make_async_copy(sketch.at[pl.ds(column(k), CHUNK)], sketch_here.at[k], sketch_done.at[k])

    for k in range(8):
        sketch_copy(k).start()
        if k < depth:
            slab_copy(k).start()
    for k in range(8):
        slab_copy(k).wait()
        sketch_copy(k).wait()
        slab_high, slab_low = halves(slab_here[k % depth])
        if k < 4:
            sent_high[k], sent_low[k] = slab_high, slab_low
        else:
            high[k - 4], low[k - 4] = slab_high, slab_low
        sketch_high, sketch_low = halves(sketch_here[k])
        both = mul(slab_high, jnp.concatenate([sketch_high, sketch_low], axis=1))
        value = both[:, :K] + (both[:, K:] + mul(slab_low, sketch_high))
        if k == 0:
            sampled[...] = value
        else:
            sampled[...] += value
        if k + depth < 8:
            slab_copy(k + depth).start()
    left[...] = jnp.concatenate(halves(sampled[...].T), axis=0)
    product(0, 1 - side, left, sent_high, sent_low, xs)


def sample(slab, sketch):
    rows = slab.shape[0]
    depth = 5
    return pl.pallas_call(
        sample_kernel,
        in_specs=[HBM, HBM],
        out_specs=[VMEM] * 7,
        out_shape=[
            jax.ShapeDtypeStruct((rows, K), F32),
            jax.ShapeDtypeStruct((2 * K, rows), BF16),
            *[jax.ShapeDtypeStruct((4, rows, CHUNK), BF16)] * 4,
            jax.ShapeDtypeStruct((4 * K, WIDTH[0]), F32),
        ],
        scratch_shapes=[
            pltpu.VMEM((depth, rows, CHUNK), F32),
            pltpu.VMEM((8, CHUNK, K), F32),
            pltpu.SemaphoreType.DMA((depth,)),
            pltpu.SemaphoreType.DMA((8,)),
        ],
        compiler_params=pltpu.CompilerParams(vmem_limit_bytes=34 * MIB),
        cost_estimate=pl.CostEstimate(flops=8 * 10**9, bytes_accessed=21 * MIB, transcendentals=0),
        name="sample",
    )(slab, sketch)


def rest_kernel(left, high, low, after, y, z):
    _, side = here()
    product(1, 1 - side, left, high, low, y)
    square = lax.dot_general(left[...], left[...], (((1,), (1,)), ((), ())), preferred_element_type=F32)
    gram = (square[:K, :K] + square[K:, K:]) + (square[:K, K:] + square[K:, :K])
    z[4 * K :] = jnp.concatenate([gram[:GRAM], gram[GRAM:]], axis=1)
    product(2, 1 - side, left, high, low, z)


def rest_to_send(left, high, low, after):
    return pl.pallas_call(
        rest_kernel,
        in_specs=[VMEM] * 3 + [pl.BlockSpec(memory_space=pl.ANY)],
        out_specs=[VMEM] * 2,
        out_shape=[
            jax.ShapeDtypeStruct((4 * K, WIDTH[1]), F32),
            jax.ShapeDtypeStruct((4 * K + GRAM, WIDTH[2]), F32),
        ],
        compiler_params=pltpu.CompilerParams(vmem_limit_bytes=20 * MIB),
        cost_estimate=pl.CostEstimate(flops=15 * 10**8, bytes_accessed=MIB, transcendentals=0),
        name="rest_to_send",
    )(left, high, low, after)


def keep_kernel(chain, left, high, low, *rest):
    _, side = here()
    out = rest[-1]
    if len(rest) > 2:
        out[4 * K :] = rest[0][4 * K :]
    product(chain, side, left, high, low, out)


def keep(chain, left, high, low, sent, after):
    rows, width = sent.shape
    args = [left, high, low] + ([sent] if rows > 4 * K else []) + [after]
    return pl.pallas_call(
        lambda *refs: keep_kernel(chain, *refs),
        in_specs=[VMEM] * (len(args) - 1) + [pl.BlockSpec(memory_space=pl.ANY)],
        out_specs=VMEM,
        out_shape=jax.ShapeDtypeStruct((rows, width), F32),
        compiler_params=pltpu.CompilerParams(vmem_limit_bytes=20 * MIB),
        cost_estimate=pl.CostEstimate(flops=7 * 10**8, bytes_accessed=MIB, transcendentals=0),
        name="keep",
    )(*args)


def diagonal_mask():
    row = lax.broadcasted_iota(jnp.int32, (K, K), 0)
    return row == lax.broadcasted_iota(jnp.int32, (K, K), 1)


def eliminate(lefts, rights, starts):
    sub = lax.broadcasted_iota(jnp.int32, (8, K), 0)
    for start in starts:
        tile, at = divmod(start, 8)
        columns = [
            [jnp.broadcast_to(lefts[t][:, start + k : start + k + 1], (8, K)) for t in range(tile, 16)]
            for k in range(AHEAD)
        ]
        rows_left = [jnp.broadcast_to(lefts[tile][at + k : at + k + 1], (8, K)) for k in range(AHEAD)]
        rows_right = [jnp.broadcast_to(rights[tile][at + k : at + k + 1], (8, K)) for k in range(AHEAD)]

        def entry(r, c):
            return jnp.broadcast_to(columns[c][0][at + r : at + r + 1], (8, K))

        for k in range(AHEAD):
            down = 1.0 / entry(k, k)
            below = [entry(m, k) for m in range(k + 1, AHEAD)]
            rows_left[k] = rows_left[k] * down
            rows_right[k] = rows_right[k] * down
            for m in range(k + 1, AHEAD):
                rows_left[m] = rows_left[m] - below[m - k - 1] * rows_left[k]
                rows_right[m] = rows_right[m] - below[m - k - 1] * rows_right[k]
                share = below[m - k - 1] * down
                columns[m] = [own - other * share for own, other in zip(columns[m], columns[k])]
        for k in range(AHEAD):
            columns[k][0] = jnp.where(sub > at + k, columns[k][0], 0.0)
        for t in range(tile, 16):
            for k in range(AHEAD):
                lefts[t] = lefts[t] - columns[k][t - tile] * rows_left[k]
                rights[t] = rights[t] - columns[k][t - tile] * rows_right[k]


def tiles_of(value):
    return [value[8 * t : 8 * t + 8] for t in range(16)]


def factor_part(state, panels, after):
    starts = range(panels[0] * AHEAD, panels[1] * AHEAD, AHEAD)
    last = panels[1] * AHEAD == K

    def body(*refs):
        if len(state) == 1:
            folded = refs[0]
            left = jnp.concatenate([folded[:, :K], folded[:, K:]], axis=0)
            right = jnp.where(diagonal_mask(), 1.0, 0.0).astype(F32)
        else:
            left, right = refs[0][...], refs[1][...]
        lefts, rights = tiles_of(left), tiles_of(right)
        eliminate(lefts, rights, starts)
        left, right = jnp.concatenate(lefts, axis=0), jnp.concatenate(rights, axis=0)
        if last:
            diagonal = jnp.sum(jnp.where(diagonal_mask(), left, 0.0), axis=1, keepdims=True)
            refs[-1][...] = right * lax.rsqrt(diagonal)
        else:
            refs[-2][...] = left
            refs[-1][...] = right

    return call_in_turn(body, list(state), [(K, K)] * (1 if last else 2), after, "factor_part", 4 * MIB, 10**9)


def call_in_turn(body, args, shapes, after, name, limit=MIB, flops=10**8):
    extra = [] if after is None else [after]
    any_space = pl.BlockSpec(memory_space=pl.ANY)

    def kernel(*refs):
        body(*refs[: len(args)], *refs[len(args) + len(extra) :])

    return pl.pallas_call(
        kernel,
        in_specs=[VMEM] * len(args) + [any_space] * len(extra),
        out_specs=[VMEM] * len(shapes),
        out_shape=[jax.ShapeDtypeStruct(shape, F32) for shape in shapes],
        compiler_params=pltpu.CompilerParams(vmem_limit_bytes=limit),
        cost_estimate=pl.CostEstimate(flops=flops, bytes_accessed=MIB // 4, transcendentals=0),
        name=name,
    )(*args, *extra)


def split(total, rest, keep, hand):
    half = keep.shape[0]
    keep[...] = total[:half]
    hand[:half] = total[half:]
    if rest is not None:
        hand[half:] = rest


def sum_cores(kept, got, after):
    rows, width = kept.shape

    def body(kept_ref, got_ref, keep, hand):
        rest = kept_ref[4 * K :] + got_ref[4 * K :] if rows > 4 * K else None
        split(kept_ref[: 4 * K] + got_ref[: 4 * K], rest, keep, hand)

    return call_in_turn(body, [kept, got], [(2 * K, width), (rows - 2 * K, width)], after, "sum_cores")


def sum_half(kept, handed, got, after):
    half, width = kept.shape
    rest = handed.shape[0] - half

    def total(kept_ref, handed_ref, got_ref):
        more = handed_ref[half:] + got_ref[half:] if rest else None
        return kept_ref[...] + got_ref[:half], more

    def halve(kept_ref, handed_ref, got_ref, keep, hand):
        split(*total(kept_ref, handed_ref, got_ref), keep, hand)

    def finish(kept_ref, handed_ref, got_ref, out):
        value, more = total(kept_ref, handed_ref, got_ref)
        out[:half] = value
        if rest:
            out[half:] = more

    args = [kept, handed, got]
    if half == K:
        return call_in_turn(finish, args, [(half + rest, width)], after, "sum_quarter")[0]
    return call_in_turn(halve, args, [(half // 2, width), (half // 2 + rest, width)], after, "sum_half")


def sum_whole(state, got, after):
    def body(state_ref, got_ref, out):
        out[...] = state_ref[...] + got_ref[...]

    return call_in_turn(body, [state, got], [state.shape], after, "sum_whole")[0]


def sum_last(state, got, after):
    rows, width = state.shape

    def body(state_ref, got_ref, own, *rest):
        own[...] = state_ref[:K] + got_ref[:K]
        if rest:
            rest[0][...] = state_ref[K:] + got_ref[K:]

    shapes = [(K, width)] + ([(rows - K, width)] if rows > K else [])
    return call_in_turn(body, [state, got], shapes, after, "sum_last")


def join(own, got, after):
    rows, width = own.shape

    def body(own_ref, got_ref, out):
        out[:rows] = own_ref[...]
        out[rows:] = got_ref[...]

    return call_in_turn(body, [own, got], [(2 * rows, width)], after, "join")[0]


def pass_on(value, after):
    any_space = pl.BlockSpec(memory_space=pl.ANY)
    return pl.pallas_call(
        lambda *refs: None,
        in_specs=[any_space] * 2,
        out_specs=any_space,
        out_shape=jax.ShapeDtypeStruct(value.shape, value.dtype),
        input_output_aliases={0: 0},
        compiler_params=pltpu.CompilerParams(vmem_limit_bytes=MIB),
        name="pass_on",
    )(value, after)


def put_products(pieces, arrays, inverse, out, ready, done):
    place, side = here()
    high, low = halves(inverse[...])
    wide = jnp.concatenate([high, high], axis=1)
    copies = []
    filled = [0, 0, 0]
    for array, (chain, other, first) in zip(arrays, pieces):
        owner = 1 - side if other else side
        width = WIDTH[chain]
        for i in range(2):
            value_high, value_low = halves(array[K * i : K * i + K])
            at = filled[chain]
            filled[chain] += 1
            stacked = jnp.concatenate([value_high, value_low], axis=0)
            ready[chain][at] = mul(wide, stacked) + mul(low, value_high)
            quarter = place[chain] ^ two_bits(QUARTERS, owner ^ FLIP[chain], first + i)
            column = pl.multiple_of(owner * HALF + STARTS[chain] + quarter * width, K)
            copies.append(
                pltpu.make_async_copy(ready[chain].at[at], out.at[:, pl.ds(column, width)], done.at[len(copies)])
            )
            copies[-1].start()
    return copies


def apply_first_kernel(pieces, scale, inverse, sampled, *rest):
    arrays, (out, basis, mark, *ready, basis_ready, done, basis_done) = rest[: len(pieces)], rest[len(pieces) :]
    mark[...] = jnp.zeros_like(mark)
    copies = put_products(pieces, arrays, inverse, out, ready, done)
    across_high, across_low = halves(inverse[...].T)
    high, low = halves(sampled[...])
    wide = jnp.concatenate([across_high, across_high], axis=0)
    basis_ready[...] = scale * (mul(jnp.concatenate([high, low], axis=1), wide) + mul(high, across_low))
    copies.append(pltpu.make_async_copy(basis_ready, basis, basis_done))
    copies[-1].start()
    for copy in copies:
        copy.wait()


def apply_next_kernel(pieces, inverse, *rest):
    arrays, (_, out, *ready, done) = rest[: len(pieces)], rest[len(pieces) :]
    for copy in put_products(pieces, arrays, inverse, out, ready, done):
        copy.wait()


def apply_scratch(pieces):
    most = [2 * sum(piece[0] == chain for piece in pieces) for chain in range(3)]
    return [pltpu.VMEM((most[chain], K, WIDTH[chain]), F32) for chain in range(3)]


def apply_first(inverse, parts, pieces, sampled, scale):
    return pl.pallas_call(
        lambda *refs: apply_first_kernel(pieces, scale, *refs),
        in_specs=[VMEM] * (2 + len(parts)),
        out_specs=[HBM, HBM, VMEM],
        out_shape=[
            jax.ShapeDtypeStruct((K, 2 * HALF), F32),
            jax.ShapeDtypeStruct(sampled.shape, F32),
            jax.ShapeDtypeStruct((8, K), F32),
        ],
        scratch_shapes=[
            *apply_scratch(pieces),
            pltpu.VMEM(sampled.shape, F32),
            pltpu.SemaphoreType.DMA((2 * len(pieces),)),
            pltpu.SemaphoreType.DMA,
        ],
        compiler_params=pltpu.CompilerParams(vmem_limit_bytes=12 * MIB),
        cost_estimate=pl.CostEstimate(flops=10**9, bytes_accessed=2 * MIB, transcendentals=0),
        name="apply_first",
    )(inverse, sampled, *parts)


def apply_next(inverse, parts, pieces, before):
    return pl.pallas_call(
        lambda *refs: apply_next_kernel(pieces, *refs),
        in_specs=[VMEM] * (1 + len(parts)) + [HBM],
        out_specs=HBM,
        out_shape=jax.ShapeDtypeStruct((K, 2 * HALF), F32),
        scratch_shapes=[*apply_scratch(pieces), pltpu.SemaphoreType.DMA((2 * len(pieces),))],
        input_output_aliases={1 + len(parts): 0},
        compiler_params=pltpu.CompilerParams(vmem_limit_bytes=12 * MIB),
        cost_estimate=pl.CostEstimate(flops=10**9, bytes_accessed=2 * MIB, transcendentals=0),
        name="apply_next",
    )(inverse, *parts, before)


def send(value, pairs):
    return lax.ppermute(value, AXES, pairs)


def per_device(slab, sketch):
    total_rows = slab.shape[0] * lax.axis_size("row") * lax.axis_size("col")
    turns = (0, 1, 2)
    sampled, left, sent_high, sent_low, high, low, first = sample(slab, sketch)
    sent = [first, *rest_to_send(left, sent_high, sent_low, first)]
    after = sent[2]
    kept, handed, states, near, far = [None] * 3, [None] * 3, [None] * 3, [None] * 3, [None] * 3
    for chain in turns:
        got = send(sent[chain], CORE_PAIRS)
        own = keep(chain, left, high, low, sent[chain], after)
        kept[chain], handed[chain] = sum_cores(own, got, None)
        after = kept[chain]
    for chain in turns:
        got = send(handed[chain], ring_pairs(chain, 0, FLIP[chain]))
        kept[chain], handed[chain] = sum_half(kept[chain], handed[chain], got, after)
        after = kept[chain]
    for chain in turns:
        got = send(handed[chain], ring_pairs(chain, 1, FLIP[chain]))
        states[chain] = after = sum_half(kept[chain], handed[chain], got, after)
    for turn, step in ((1, 0), (1, 1), (2, 0)):
        for chain in turns:
            got = send(states[chain], ring_pairs((chain + turn) % 3, step, FLIP[chain]))
            states[chain] = after = sum_whole(states[chain], got, after)
    gram = None
    for chain in turns:
        got = send(states[chain], ring_pairs((chain + 2) % 3, 1, FLIP[chain]))
        states[chain], *rest = sum_last(states[chain], got, after)
        after = states[chain]
        gram = rest[0] if rest else gram
    state = [gram]
    for chain, panels in zip(turns, ((0, 2), (2, 4), (4, 6))):
        state = factor_part(state, panels, after)
        got = send(states[chain], ring_pairs(chain, 1, FLIP[chain]))
        near[chain] = after = join(states[chain], got, state[0])
    (inverse,) = factor_part(state, (6, 16), after)
    scale = math.sqrt(total_rows)
    out, basis, mark = apply_first(inverse, near, [(a, 0, 0) for a in range(3)], sampled, scale)
    near_other = [send(pass_on(part, mark), CORE_PAIRS) for part in near]
    for chain in turns:
        far[chain] = pass_on(send(near[chain], ring_pairs(chain, 0, FLIP[chain])), mark)
    far_other = [send(part, CORE_PAIRS) for part in far]
    middle = [(a, 0, 2) for a in range(3)] + [(a, 1, 0) for a in range(3)]
    out = apply_next(inverse, far + near_other, middle, out)
    out = apply_next(inverse, far_other, [(a, 1, 2) for a in range(3)], out)
    return basis, out


def solution(mesh):
    return jax.shard_map(
        per_device,
        mesh=mesh,
        in_specs=(P(AXES, None), P()),
        out_specs=(P(AXES, None), P()),
        check_vma=False,
    )
```

```python
import math

import jax
import jax.numpy as jnp
from jax import lax
from jax.experimental import pallas as pl
from jax.experimental.pallas import tpu as pltpu
from jax.sharding import PartitionSpec as P

AXES = ("row", "col")
RING = 4
K = 128
CHUNK = 1024
HALF = 4096
WIDTH = (384, 384, 256)
STARTS = (0, 1536, 3072)
GRAM = 64
FLIP = (0, 1, 0)
AHEAD = 8
QUARTERS = (156, 180)
SLOTS = (120, 180)
MIB = 2**20
F32 = jnp.float32
BF16 = jnp.bfloat16
HIGHEST = lax.Precision.HIGHEST
VMEM = pl.BlockSpec(memory_space=pltpu.VMEM)
HBM = pl.BlockSpec(memory_space=pltpu.HBM)


def places():
    return [
        (x, y, z, c) for y in range(RING) for c in range(2) for x in range(RING) for z in range(RING)
    ]


def linear(x, y, z, c):
    return (y * 2 + c) * RING * RING + x * RING + z


def side_of(x, y, z, core):
    return core ^ ((x + y + z) & 1)


def beside(place, step, side):
    return place ^ 1 if (step ^ side) == 0 else place ^ 3


def ring_pairs(axis, step, flip=0):
    pairs = []
    for x, y, z, c in places():
        to = [x, y, z]
        to[axis] = beside(to[axis], step ^ flip, side_of(x, y, z, c))
        pairs.append((linear(x, y, z, c), linear(*to, 1 - c)))
    return pairs


CORE_PAIRS = [(linear(x, y, z, c), linear(x, y, z, 1 - c)) for x, y, z, c in places()]


def here():
    row, col = lax.axis_index("row"), lax.axis_index("col")
    place = (col // RING, row // 2, col % RING)
    return place, side_of(*place, row % 2)


def two_bits(choices, side, at):
    return (jnp.where(side == 0, choices[0], choices[1]) >> (2 * at)) & 3


def halves(value):
    high = value.astype(BF16)
    return high, (value - high.astype(F32)).astype(BF16)


def mul(a, b):
    return jnp.dot(a, b, preferred_element_type=F32)


def product(chain, side, left, high, low, out):
    place, _ = here()
    width = WIDTH[chain]
    for i in range(4):
        first = max(STARTS[chain], i * CHUNK)
        last = min(STARTS[chain] + 4 * width, (i + 1) * CHUNK)
        if first >= last:
            continue
        at = slice(first - i * CHUNK, last - i * CHUNK)
        both = mul(left[...], high[i, :, at])
        value = both[:K] + (both[K:] + mul(left[:K], low[i, :, at]))
        begin = first
        while begin < last:
            quarter, within = divmod(begin - STARTS[chain], width)
            size = min(width - within, last - begin)
            slot = two_bits(SLOTS, side ^ FLIP[chain], quarter ^ place[chain])
            rows = pl.ds(pl.multiple_of(slot * K, K), K)
            out[rows, within : within + size] = value[:, begin - first : begin - first + size]
            begin += size


def sample_kernel(
    slab, sketch, sampled, left, sent_high, sent_low, high, low, xs,
    slab_here, sketch_here, slab_done, sketch_done,
):
    _, side = here()
    depth = slab_here.shape[0]

    def column(k):
        half = 1 - side if k < 4 else side
        return pl.multiple_of(half * HALF + (k % 4) * CHUNK, CHUNK)

    def slab_copy(k):
        return pltpu.make_async_copy(
            slab.at[:, pl.ds(column(k), CHUNK)], slab_here.at[k % depth], slab_done.at[k % depth]
        )

    def sketch_copy(k):
        return pltpu.make_async_copy(sketch.at[pl.ds(column(k), CHUNK)], sketch_here.at[k], sketch_done.at[k])

    for k in range(8):
        sketch_copy(k).start()
        if k < depth:
            slab_copy(k).start()
    for k in range(8):
        slab_copy(k).wait()
        sketch_copy(k).wait()
        slab_high, slab_low = halves(slab_here[k % depth])
        if k < 4:
            sent_high[k], sent_low[k] = slab_high, slab_low
        else:
            at = pl.ds((k - 4) * CHUNK, CHUNK)
            high[:, at], low[:, at] = slab_high, slab_low
        sketch_high, sketch_low = halves(sketch_here[k])
        both = mul(slab_high, jnp.concatenate([sketch_high, sketch_low], axis=1))
        value = both[:, :K] + (both[:, K:] + mul(slab_low, sketch_high))
        if k == 0:
            sampled[...] = value
        else:
            sampled[...] += value
        if k + depth < 8:
            slab_copy(k + depth).start()
    left[...] = jnp.concatenate(halves(sampled[...].T), axis=0)
    product(0, 1 - side, left, sent_high, sent_low, xs)


def sample(slab, sketch):
    rows = slab.shape[0]
    depth = 5
    return pl.pallas_call(
        sample_kernel,
        in_specs=[HBM, HBM],
        out_specs=[VMEM] * 7,
        out_shape=[
            jax.ShapeDtypeStruct((rows, K), F32),
            jax.ShapeDtypeStruct((2 * K, rows), BF16),
            *[jax.ShapeDtypeStruct((4, rows, CHUNK), BF16)] * 2,
            *[jax.ShapeDtypeStruct((rows, HALF), BF16)] * 2,
            jax.ShapeDtypeStruct((4 * K, WIDTH[0]), F32),
        ],
        scratch_shapes=[
            pltpu.VMEM((depth, rows, CHUNK), F32),
            pltpu.VMEM((8, CHUNK, K), F32),
            pltpu.SemaphoreType.DMA((depth,)),
            pltpu.SemaphoreType.DMA((8,)),
        ],
        compiler_params=pltpu.CompilerParams(vmem_limit_bytes=34 * MIB),
        cost_estimate=pl.CostEstimate(flops=8 * 10**9, bytes_accessed=21 * MIB, transcendentals=0),
        name="sample",
    )(slab, sketch)


def rest_kernel(left, high, low, after, y, z):
    _, side = here()
    product(1, 1 - side, left, high, low, y)
    square = lax.dot_general(left[...], left[...], (((1,), (1,)), ((), ())), preferred_element_type=F32)
    gram = (square[:K, :K] + square[K:, K:]) + (square[:K, K:] + square[K:, :K])
    z[4 * K :] = jnp.concatenate([gram[:GRAM], gram[GRAM:]], axis=1)
    product(2, 1 - side, left, high, low, z)


def rest_to_send(left, high, low, after):
    return pl.pallas_call(
        rest_kernel,
        in_specs=[VMEM] * 3 + [pl.BlockSpec(memory_space=pl.ANY)],
        out_specs=[VMEM] * 2,
        out_shape=[
            jax.ShapeDtypeStruct((4 * K, WIDTH[1]), F32),
            jax.ShapeDtypeStruct((4 * K + GRAM, WIDTH[2]), F32),
        ],
        compiler_params=pltpu.CompilerParams(vmem_limit_bytes=20 * MIB),
        cost_estimate=pl.CostEstimate(flops=15 * 10**8, bytes_accessed=MIB, transcendentals=0),
        name="rest_to_send",
    )(left, high, low, after)


def own_kernel(chain, slots, left, high, low, *rest):
    place, side = here()
    out = rest[-1]
    width = WIDTH[chain]
    if len(rest) > 2:
        out[2 * K :] = rest[0][4 * K :]
    for i, slot in enumerate(slots):
        quarter = place[chain] ^ two_bits(QUARTERS, side ^ FLIP[chain], slot)
        at = pl.ds(pl.multiple_of(STARTS[chain] + quarter * width, K), width)
        both = mul(left[...], high[:, at])
        out[K * i : K * i + K] = both[:K] + (both[K:] + mul(left[:K], low[:, at]))


def own_part(chain, slots, left, high, low, sent, after):
    args = [left, high, low] + ([] if sent is None else [sent]) + [after]
    rows = 2 * K + (0 if sent is None else GRAM)
    return pl.pallas_call(
        lambda *refs: own_kernel(chain, slots, *refs),
        in_specs=[VMEM] * (len(args) - 1) + [pl.BlockSpec(memory_space=pl.ANY)],
        out_specs=VMEM,
        out_shape=jax.ShapeDtypeStruct((rows, WIDTH[chain]), F32),
        compiler_params=pltpu.CompilerParams(vmem_limit_bytes=20 * MIB),
        cost_estimate=pl.CostEstimate(flops=7 * 10**8, bytes_accessed=MIB, transcendentals=0),
        name="own_part",
    )(*args)


def diagonal_mask():
    row = lax.broadcasted_iota(jnp.int32, (K, K), 0)
    return row == lax.broadcasted_iota(jnp.int32, (K, K), 1)


def eliminate(lefts, rights, starts):
    sub = lax.broadcasted_iota(jnp.int32, (8, K), 0)
    for start in starts:
        tile, at = divmod(start, 8)
        columns = [
            [jnp.broadcast_to(lefts[t][:, start + k : start + k + 1], (8, K)) for t in range(tile, 16)]
            for k in range(AHEAD)
        ]
        rows_left = [jnp.broadcast_to(lefts[tile][at + k : at + k + 1], (8, K)) for k in range(AHEAD)]
        rows_right = [jnp.broadcast_to(rights[tile][at + k : at + k + 1], (8, K)) for k in range(AHEAD)]

        def entry(r, c):
            return jnp.broadcast_to(columns[c][0][at + r : at + r + 1], (8, K))

        for k in range(AHEAD):
            down = 1.0 / entry(k, k)
            below = [entry(m, k) for m in range(k + 1, AHEAD)]
            rows_left[k] = rows_left[k] * down
            rows_right[k] = rows_right[k] * down
            for m in range(k + 1, AHEAD):
                rows_left[m] = rows_left[m] - below[m - k - 1] * rows_left[k]
                rows_right[m] = rows_right[m] - below[m - k - 1] * rows_right[k]
                share = below[m - k - 1] * down
                columns[m] = [own - other * share for own, other in zip(columns[m], columns[k])]
        for k in range(AHEAD):
            columns[k][0] = jnp.where(sub > at + k, columns[k][0], 0.0)
        for t in range(tile, 16):
            for k in range(AHEAD):
                lefts[t] = lefts[t] - columns[k][t - tile] * rows_left[k]
                rights[t] = rights[t] - columns[k][t - tile] * rows_right[k]


def tiles_of(value):
    return [value[8 * t : 8 * t + 8] for t in range(16)]


def factor_part(state, panels, after):
    starts = range(panels[0] * AHEAD, panels[1] * AHEAD, AHEAD)
    last = panels[1] * AHEAD == K

    def body(*refs):
        if len(state) == 1:
            folded = refs[0]
            left = jnp.concatenate([folded[:, :K], folded[:, K:]], axis=0)
            right = jnp.where(diagonal_mask(), 1.0, 0.0).astype(F32)
        else:
            left, right = refs[0][...], refs[1][...]
        lefts, rights = tiles_of(left), tiles_of(right)
        eliminate(lefts, rights, starts)
        left, right = jnp.concatenate(lefts, axis=0), jnp.concatenate(rights, axis=0)
        if last:
            diagonal = jnp.sum(jnp.where(diagonal_mask(), left, 0.0), axis=1, keepdims=True)
            refs[-1][...] = right * lax.rsqrt(diagonal)
        else:
            refs[-2][...] = left
            refs[-1][...] = right

    return call_in_turn(body, list(state), [(K, K)] * (1 if last else 2), after, "factor_part", 4 * MIB, 10**9)


def call_in_turn(body, args, shapes, after, name, limit=MIB, flops=10**8):
    extra = [] if after is None else [after]
    any_space = pl.BlockSpec(memory_space=pl.ANY)

    def kernel(*refs):
        body(*refs[: len(args)], *refs[len(args) + len(extra) :])

    return pl.pallas_call(
        kernel,
        in_specs=[VMEM] * len(args) + [any_space] * len(extra),
        out_specs=[VMEM] * len(shapes),
        out_shape=[jax.ShapeDtypeStruct(shape, F32) for shape in shapes],
        compiler_params=pltpu.CompilerParams(vmem_limit_bytes=limit),
        cost_estimate=pl.CostEstimate(flops=flops, bytes_accessed=MIB // 4, transcendentals=0),
        name=name,
    )(*args, *extra)


def split(total, rest, keep, hand):
    half = keep.shape[0]
    keep[...] = total[:half]
    hand[:half] = total[half:]
    if rest is not None:
        hand[half:] = rest


def sum_handed(own, got, after):
    def body(own_ref, got_ref, out):
        out[...] = own_ref[...] + got_ref[2 * K :]

    return call_in_turn(body, [own, got], [own.shape], after, "sum_handed")[0]


def sum_kept(own, got, after):
    def body(own_ref, got_ref, out):
        out[...] = own_ref[...] + got_ref[: 2 * K]

    return call_in_turn(body, [own, got], [own.shape], after, "sum_kept")[0]


def sum_half(kept, handed, got, after):
    half, width = kept.shape
    rest = handed.shape[0] - half

    def total(kept_ref, handed_ref, got_ref):
        more = handed_ref[half:] + got_ref[half:] if rest else None
        return kept_ref[...] + got_ref[:half], more

    def halve(kept_ref, handed_ref, got_ref, keep, hand):
        split(*total(kept_ref, handed_ref, got_ref), keep, hand)

    def finish(kept_ref, handed_ref, got_ref, out):
        value, more = total(kept_ref, handed_ref, got_ref)
        out[:half] = value
        if rest:
            out[half:] = more

    args = [kept, handed, got]
    if half == K:
        return call_in_turn(finish, args, [(half + rest, width)], after, "sum_quarter")[0]
    return call_in_turn(halve, args, [(half // 2, width), (half // 2 + rest, width)], after, "sum_half")


def sum_whole(state, got, after):
    def body(state_ref, got_ref, out):
        out[...] = state_ref[...] + got_ref[...]

    return call_in_turn(body, [state, got], [state.shape], after, "sum_whole")[0]


def sum_last(state, got, after):
    rows, width = state.shape

    def body(state_ref, got_ref, own, *rest):
        own[...] = state_ref[:K] + got_ref[:K]
        if rest:
            rest[0][...] = state_ref[K:] + got_ref[K:]

    shapes = [(K, width)] + ([(rows - K, width)] if rows > K else [])
    return call_in_turn(body, [state, got], shapes, after, "sum_last")


def join(own, got, after):
    rows, width = own.shape

    def body(own_ref, got_ref, out):
        out[:rows] = own_ref[...]
        out[rows:] = got_ref[...]

    return call_in_turn(body, [own, got], [(2 * rows, width)], after, "join")[0]


def pass_on(value, after):
    any_space = pl.BlockSpec(memory_space=pl.ANY)
    return pl.pallas_call(
        lambda *refs: None,
        in_specs=[any_space] * 2,
        out_specs=any_space,
        out_shape=jax.ShapeDtypeStruct(value.shape, value.dtype),
        input_output_aliases={0: 0},
        compiler_params=pltpu.CompilerParams(vmem_limit_bytes=MIB),
        name="pass_on",
    )(value, after)


def put_products(pieces, arrays, inverse, out, ready, done):
    place, side = here()
    high, low = halves(inverse[...])
    wide = jnp.concatenate([high, high], axis=1)
    copies = []
    filled = [0, 0, 0]
    for array, (chain, other, first) in zip(arrays, pieces):
        owner = 1 - side if other else side
        width = WIDTH[chain]
        for i in range(2):
            value_high, value_low = halves(array[K * i : K * i + K])
            at = filled[chain]
            filled[chain] += 1
            stacked = jnp.concatenate([value_high, value_low], axis=0)
            ready[chain][at] = mul(wide, stacked) + mul(low, value_high)
            quarter = place[chain] ^ two_bits(QUARTERS, owner ^ FLIP[chain], first + i)
            column = pl.multiple_of(owner * HALF + STARTS[chain] + quarter * width, K)
            copies.append(
                pltpu.make_async_copy(ready[chain].at[at], out.at[:, pl.ds(column, width)], done.at[len(copies)])
            )
            copies[-1].start()
    return copies


def apply_first_kernel(pieces, scale, inverse, sampled, *rest):
    arrays, (out, basis, mark, *ready, basis_ready, done, basis_done) = rest[: len(pieces)], rest[len(pieces) :]
    mark[...] = jnp.zeros_like(mark)
    copies = put_products(pieces, arrays, inverse, out, ready, done)
    across_high, across_low = halves(inverse[...].T)
    high, low = halves(sampled[...])
    wide = jnp.concatenate([across_high, across_high], axis=0)
    basis_ready[...] = scale * (mul(jnp.concatenate([high, low], axis=1), wide) + mul(high, across_low))
    copies.append(pltpu.make_async_copy(basis_ready, basis, basis_done))
    copies[-1].start()
    for copy in copies:
        copy.wait()


def apply_next_kernel(pieces, inverse, *rest):
    arrays, (_, out, *ready, done) = rest[: len(pieces)], rest[len(pieces) :]
    for copy in put_products(pieces, arrays, inverse, out, ready, done):
        copy.wait()


def apply_scratch(pieces):
    most = [2 * sum(piece[0] == chain for piece in pieces) for chain in range(3)]
    return [pltpu.VMEM((most[chain], K, WIDTH[chain]), F32) for chain in range(3)]


def apply_first(inverse, parts, pieces, sampled, scale):
    return pl.pallas_call(
        lambda *refs: apply_first_kernel(pieces, scale, *refs),
        in_specs=[VMEM] * (2 + len(parts)),
        out_specs=[HBM, HBM, VMEM],
        out_shape=[
            jax.ShapeDtypeStruct((K, 2 * HALF), F32),
            jax.ShapeDtypeStruct(sampled.shape, F32),
            jax.ShapeDtypeStruct((8, K), F32),
        ],
        scratch_shapes=[
            *apply_scratch(pieces),
            pltpu.VMEM(sampled.shape, F32),
            pltpu.SemaphoreType.DMA((2 * len(pieces),)),
            pltpu.SemaphoreType.DMA,
        ],
        compiler_params=pltpu.CompilerParams(vmem_limit_bytes=12 * MIB),
        cost_estimate=pl.CostEstimate(flops=10**9, bytes_accessed=2 * MIB, transcendentals=0),
        name="apply_first",
    )(inverse, sampled, *parts)


def apply_next(inverse, parts, pieces, before):
    return pl.pallas_call(
        lambda *refs: apply_next_kernel(pieces, *refs),
        in_specs=[VMEM] * (1 + len(parts)) + [HBM],
        out_specs=HBM,
        out_shape=jax.ShapeDtypeStruct((K, 2 * HALF), F32),
        scratch_shapes=[*apply_scratch(pieces), pltpu.SemaphoreType.DMA((2 * len(pieces),))],
        input_output_aliases={1 + len(parts): 0},
        compiler_params=pltpu.CompilerParams(vmem_limit_bytes=12 * MIB),
        cost_estimate=pl.CostEstimate(flops=10**9, bytes_accessed=2 * MIB, transcendentals=0),
        name="apply_next",
    )(inverse, *parts, before)


def send(value, pairs):
    return lax.ppermute(value, AXES, pairs)


def per_device(slab, sketch):
    total_rows = slab.shape[0] * lax.axis_size("row") * lax.axis_size("col")
    turns = (0, 1, 2)
    sampled, left, sent_high, sent_low, high, low, first = sample(slab, sketch)
    sent = [first, *rest_to_send(left, sent_high, sent_low, first)]
    after = sent[2]
    kept, handed, states, near, far = [None] * 3, [None] * 3, [None] * 3, [None] * 3, [None] * 3
    cores = [None] * 3
    for chain in turns:
        cores[chain] = send(sent[chain], CORE_PAIRS)
        own = own_part(chain, (2, 3), left, high, low, sent[2] if chain == 2 else None, after)
        handed[chain] = after = sum_handed(own, cores[chain], None)
    for chain in turns:
        own = own_part(chain, (0, 1), left, high, low, None, after)
        kept[chain] = after = sum_kept(own, cores[chain], None)
    for chain in turns:
        got = send(handed[chain], ring_pairs(chain, 0, FLIP[chain]))
        kept[chain], handed[chain] = sum_half(kept[chain], handed[chain], got, after)
        after = kept[chain]
    for chain in turns:
        got = send(handed[chain], ring_pairs(chain, 1, FLIP[chain]))
        states[chain] = after = sum_half(kept[chain], handed[chain], got, after)
    for turn, step in ((1, 0), (1, 1), (2, 0)):
        for chain in turns:
            got = send(states[chain], ring_pairs((chain + turn) % 3, step, FLIP[chain]))
            states[chain] = after = sum_whole(states[chain], got, after)
    gram = None
    for chain in turns:
        got = send(states[chain], ring_pairs((chain + 2) % 3, 1, FLIP[chain]))
        states[chain], *rest = sum_last(states[chain], got, after)
        after = states[chain]
        gram = rest[0] if rest else gram
    state = [gram]
    for chain, panels in zip(turns, ((0, 2), (2, 4), (4, 6))):
        state = factor_part(state, panels, after)
        got = send(states[chain], ring_pairs(chain, 1, FLIP[chain]))
        near[chain] = after = join(states[chain], got, state[0])
    (inverse,) = factor_part(state, (6, 16), after)
    scale = math.sqrt(total_rows)
    out, basis, mark = apply_first(inverse, near, [(a, 0, 0) for a in range(3)], sampled, scale)
    near_other = [send(pass_on(part, mark), CORE_PAIRS) for part in near]
    for chain in turns:
        far[chain] = pass_on(send(near[chain], ring_pairs(chain, 0, FLIP[chain])), mark)
    far_other = [send(part, CORE_PAIRS) for part in far]
    middle = [(a, 0, 2) for a in range(3)] + [(a, 1, 0) for a in range(3)]
    out = apply_next(inverse, far + near_other, middle, out)
    out = apply_next(inverse, far_other, [(a, 1, 2) for a in range(3)], out)
    return basis, out


def solution(mesh):
    return jax.shard_map(
        per_device,
        mesh=mesh,
        in_specs=(P(AXES, None), P()),
        out_specs=(P(AXES, None), P()),
        check_vma=False,
    )
```

```python
import math

import jax
import jax.numpy as jnp
from jax import lax
from jax.experimental import pallas as pl
from jax.experimental.pallas import tpu as pltpu
from jax.sharding import PartitionSpec as P

AXES = ("row", "col")
RING = 4
K = 128
CHUNK = 1024
HALF = 4096
WIDTH = (384, 384, 256)
STARTS = (0, 1536, 3072)
GRAM = 64
FLIP = (0, 1, 0)
AHEAD = 8
QUARTERS = (156, 180)
SLOTS = (120, 180)
MIB = 2**20
F32 = jnp.float32
BF16 = jnp.bfloat16
HIGHEST = lax.Precision.HIGHEST
VMEM = pl.BlockSpec(memory_space=pltpu.VMEM)
HBM = pl.BlockSpec(memory_space=pltpu.HBM)


def places():
    return [
        (x, y, z, c) for y in range(RING) for c in range(2) for x in range(RING) for z in range(RING)
    ]


def linear(x, y, z, c):
    return (y * 2 + c) * RING * RING + x * RING + z


def side_of(x, y, z, core):
    return core ^ ((x + y + z) & 1)


def beside(place, step, side):
    return place ^ 1 if (step ^ side) == 0 else place ^ 3


def ring_pairs(axis, step, flip=0):
    pairs = []
    for x, y, z, c in places():
        to = [x, y, z]
        to[axis] = beside(to[axis], step ^ flip, side_of(x, y, z, c))
        pairs.append((linear(x, y, z, c), linear(*to, 1 - c)))
    return pairs


CORE_PAIRS = [(linear(x, y, z, c), linear(x, y, z, 1 - c)) for x, y, z, c in places()]


def here():
    row, col = lax.axis_index("row"), lax.axis_index("col")
    place = (col // RING, row // 2, col % RING)
    return place, side_of(*place, row % 2)


def two_bits(choices, side, at):
    return (jnp.where(side == 0, choices[0], choices[1]) >> (2 * at)) & 3


def halves(value):
    high = value.astype(BF16)
    return high, (value - high.astype(F32)).astype(BF16)


def mul(a, b):
    return jnp.dot(a, b, preferred_element_type=F32)


def product(chain, side, left, high, low, out):
    place, _ = here()
    width = WIDTH[chain]
    for i in range(4):
        first = max(STARTS[chain], i * CHUNK)
        last = min(STARTS[chain] + 4 * width, (i + 1) * CHUNK)
        if first >= last:
            continue
        at = slice(first - i * CHUNK, last - i * CHUNK)
        both = mul(left[...], high[i, :, at])
        value = both[:K] + (both[K:] + mul(left[:K], low[i, :, at]))
        begin = first
        while begin < last:
            quarter, within = divmod(begin - STARTS[chain], width)
            size = min(width - within, last - begin)
            slot = two_bits(SLOTS, side ^ FLIP[chain], quarter ^ place[chain])
            rows = pl.ds(pl.multiple_of(slot * K, K), K)
            out[rows, within : within + size] = value[:, begin - first : begin - first + size]
            begin += size


def sample_kernel(
    slab, sketch, sampled, left, sent_high, sent_low, high, low, xs,
    slab_here, sketch_here, slab_done, sketch_done,
):
    _, side = here()
    depth = slab_here.shape[0]

    def column(k):
        half = 1 - side if k < 4 else side
        return pl.multiple_of(half * HALF + (k % 4) * CHUNK, CHUNK)

    def slab_copy(k):
        return pltpu.make_async_copy(
            slab.at[:, pl.ds(column(k), CHUNK)], slab_here.at[k % depth], slab_done.at[k % depth]
        )

    def sketch_copy(k):
        return pltpu.make_async_copy(sketch.at[pl.ds(column(k), CHUNK)], sketch_here.at[k], sketch_done.at[k])

    for k in range(8):
        sketch_copy(k).start()
        if k < depth:
            slab_copy(k).start()
    for k in range(8):
        slab_copy(k).wait()
        sketch_copy(k).wait()
        slab_high, slab_low = halves(slab_here[k % depth])
        if k < 4:
            sent_high[k], sent_low[k] = slab_high, slab_low
        else:
            at = pl.ds((k - 4) * CHUNK, CHUNK)
            high[:, at], low[:, at] = slab_high, slab_low
        sketch_high, sketch_low = halves(sketch_here[k])
        both = mul(slab_high, jnp.concatenate([sketch_high, sketch_low], axis=1))
        value = both[:, :K] + (both[:, K:] + mul(slab_low, sketch_high))
        if k == 0:
            sampled[...] = value
        else:
            sampled[...] += value
        if k + depth < 8:
            slab_copy(k + depth).start()
    left[...] = jnp.concatenate(halves(sampled[...].T), axis=0)
    product(0, 1 - side, left, sent_high, sent_low, xs)


def sample(slab, sketch):
    rows = slab.shape[0]
    depth = 5
    return pl.pallas_call(
        sample_kernel,
        in_specs=[HBM, HBM],
        out_specs=[VMEM] * 7,
        out_shape=[
            jax.ShapeDtypeStruct((rows, K), F32),
            jax.ShapeDtypeStruct((2 * K, rows), BF16),
            *[jax.ShapeDtypeStruct((4, rows, CHUNK), BF16)] * 2,
            *[jax.ShapeDtypeStruct((rows, HALF), BF16)] * 2,
            jax.ShapeDtypeStruct((4 * K, WIDTH[0]), F32),
        ],
        scratch_shapes=[
            pltpu.VMEM((depth, rows, CHUNK), F32),
            pltpu.VMEM((8, CHUNK, K), F32),
            pltpu.SemaphoreType.DMA((depth,)),
            pltpu.SemaphoreType.DMA((8,)),
        ],
        compiler_params=pltpu.CompilerParams(vmem_limit_bytes=34 * MIB),
        cost_estimate=pl.CostEstimate(flops=8 * 10**9, bytes_accessed=21 * MIB, transcendentals=0),
        name="sample",
    )(slab, sketch)


def rest_kernel(left, high, low, after, y, z):
    _, side = here()
    product(1, 1 - side, left, high, low, y)
    square = lax.dot_general(left[...], left[...], (((1,), (1,)), ((), ())), preferred_element_type=F32)
    gram = (square[:K, :K] + square[K:, K:]) + (square[:K, K:] + square[K:, :K])
    z[4 * K :] = jnp.concatenate([gram[:GRAM], gram[GRAM:]], axis=1)
    product(2, 1 - side, left, high, low, z)


def rest_to_send(left, high, low, after):
    return pl.pallas_call(
        rest_kernel,
        in_specs=[VMEM] * 3 + [pl.BlockSpec(memory_space=pl.ANY)],
        out_specs=[VMEM] * 2,
        out_shape=[
            jax.ShapeDtypeStruct((4 * K, WIDTH[1]), F32),
            jax.ShapeDtypeStruct((4 * K + GRAM, WIDTH[2]), F32),
        ],
        compiler_params=pltpu.CompilerParams(vmem_limit_bytes=20 * MIB),
        cost_estimate=pl.CostEstimate(flops=15 * 10**8, bytes_accessed=MIB, transcendentals=0),
        name="rest_to_send",
    )(left, high, low, after)


def own_kernel(chain, slots, left, high, low, *rest):
    place, side = here()
    out = rest[-1]
    width = WIDTH[chain]
    if len(rest) > 2:
        out[2 * K :] = rest[0][4 * K :]
    for i, slot in enumerate(slots):
        quarter = place[chain] ^ two_bits(QUARTERS, side ^ FLIP[chain], slot)
        at = pl.ds(pl.multiple_of(STARTS[chain] + quarter * width, K), width)
        both = mul(left[...], high[:, at])
        out[K * i : K * i + K] = both[:K] + (both[K:] + mul(left[:K], low[:, at]))


def own_part(chain, slots, left, high, low, sent, after):
    args = [left, high, low] + ([] if sent is None else [sent]) + [after]
    rows = 2 * K + (0 if sent is None else GRAM)
    return pl.pallas_call(
        lambda *refs: own_kernel(chain, slots, *refs),
        in_specs=[VMEM] * (len(args) - 1) + [pl.BlockSpec(memory_space=pl.ANY)],
        out_specs=VMEM,
        out_shape=jax.ShapeDtypeStruct((rows, WIDTH[chain]), F32),
        compiler_params=pltpu.CompilerParams(vmem_limit_bytes=20 * MIB),
        cost_estimate=pl.CostEstimate(flops=7 * 10**8, bytes_accessed=MIB, transcendentals=0),
        name="own_part",
    )(*args)


def diagonal_mask():
    row = lax.broadcasted_iota(jnp.int32, (K, K), 0)
    return row == lax.broadcasted_iota(jnp.int32, (K, K), 1)


def eliminate(lefts, rights, starts):
    sub = lax.broadcasted_iota(jnp.int32, (8, K), 0)
    for start in starts:
        tile, at = divmod(start, 8)
        columns = [
            [jnp.broadcast_to(lefts[t][:, start + k : start + k + 1], (8, K)) for t in range(tile, 16)]
            for k in range(AHEAD)
        ]
        rows_left = [jnp.broadcast_to(lefts[tile][at + k : at + k + 1], (8, K)) for k in range(AHEAD)]
        rows_right = [jnp.broadcast_to(rights[tile][at + k : at + k + 1], (8, K)) for k in range(AHEAD)]

        def entry(r, c):
            return jnp.broadcast_to(columns[c][0][at + r : at + r + 1], (8, K))

        for k in range(AHEAD):
            down = 1.0 / entry(k, k)
            below = [entry(m, k) for m in range(k + 1, AHEAD)]
            rows_left[k] = rows_left[k] * down
            rows_right[k] = rows_right[k] * down
            for m in range(k + 1, AHEAD):
                rows_left[m] = rows_left[m] - below[m - k - 1] * rows_left[k]
                rows_right[m] = rows_right[m] - below[m - k - 1] * rows_right[k]
                share = below[m - k - 1] * down
                columns[m] = [own - other * share for own, other in zip(columns[m], columns[k])]
        for k in range(AHEAD):
            columns[k][0] = jnp.where(sub > at + k, columns[k][0], 0.0)
        for t in range(tile, 16):
            for k in range(AHEAD):
                lefts[t] = lefts[t] - columns[k][t - tile] * rows_left[k]
                rights[t] = rights[t] - columns[k][t - tile] * rows_right[k]


def tiles_of(value):
    return [value[8 * t : 8 * t + 8] for t in range(16)]


def factor_part(state, panels, after):
    starts = range(panels[0] * AHEAD, panels[1] * AHEAD, AHEAD)
    last = panels[1] * AHEAD == K

    def body(*refs):
        if len(state) == 1:
            folded = refs[0]
            left = jnp.concatenate([folded[:, :K], folded[:, K:]], axis=0)
            right = jnp.where(diagonal_mask(), 1.0, 0.0).astype(F32)
        else:
            left, right = refs[0][...], refs[1][...]
        lefts, rights = tiles_of(left), tiles_of(right)
        eliminate(lefts, rights, starts)
        left, right = jnp.concatenate(lefts, axis=0), jnp.concatenate(rights, axis=0)
        if last:
            diagonal = jnp.sum(jnp.where(diagonal_mask(), left, 0.0), axis=1, keepdims=True)
            refs[-1][...] = right * lax.rsqrt(diagonal)
        else:
            refs[-2][...] = left
            refs[-1][...] = right

    return call_in_turn(body, list(state), [(K, K)] * (1 if last else 2), after, "factor_part", 4 * MIB, 10**9)


def call_in_turn(body, args, shapes, after, name, limit=MIB, flops=10**8):
    extra = [] if after is None else [after]
    any_space = pl.BlockSpec(memory_space=pl.ANY)

    def kernel(*refs):
        body(*refs[: len(args)], *refs[len(args) + len(extra) :])

    return pl.pallas_call(
        kernel,
        in_specs=[VMEM] * len(args) + [any_space] * len(extra),
        out_specs=[VMEM] * len(shapes),
        out_shape=[jax.ShapeDtypeStruct(shape, F32) for shape in shapes],
        compiler_params=pltpu.CompilerParams(vmem_limit_bytes=limit),
        cost_estimate=pl.CostEstimate(flops=flops, bytes_accessed=MIB // 4, transcendentals=0),
        name=name,
    )(*args, *extra)


def split(total, rest, keep, hand):
    half = keep.shape[0]
    keep[...] = total[:half]
    hand[:half] = total[half:]
    if rest is not None:
        hand[half:] = rest


def sum_handed(own, got, after):
    def body(own_ref, got_ref, out):
        out[...] = own_ref[...] + got_ref[2 * K :]

    return call_in_turn(body, [own, got], [own.shape], after, "sum_handed")[0]


def sum_kept(own, got, after):
    def body(own_ref, got_ref, out):
        out[...] = own_ref[...] + got_ref[: 2 * K]

    return call_in_turn(body, [own, got], [own.shape], after, "sum_kept")[0]


def sum_half(kept, handed, got, after):
    half, width = kept.shape
    rest = handed.shape[0] - half

    def total(kept_ref, handed_ref, got_ref):
        more = handed_ref[half:] + got_ref[half:] if rest else None
        return kept_ref[...] + got_ref[:half], more

    def halve(kept_ref, handed_ref, got_ref, keep, hand):
        split(*total(kept_ref, handed_ref, got_ref), keep, hand)

    def finish(kept_ref, handed_ref, got_ref, out):
        value, more = total(kept_ref, handed_ref, got_ref)
        out[:half] = value
        if rest:
            out[half:] = more

    args = [kept, handed, got]
    if half == K:
        return call_in_turn(finish, args, [(half + rest, width)], after, "sum_quarter")[0]
    return call_in_turn(halve, args, [(half // 2, width), (half // 2 + rest, width)], after, "sum_half")


def sum_whole(state, got, after):
    def body(state_ref, got_ref, out):
        out[...] = state_ref[...] + got_ref[...]

    return call_in_turn(body, [state, got], [state.shape], after, "sum_whole")[0]


def sum_last(state, got, after):
    rows, width = state.shape

    def body(state_ref, got_ref, own, *rest):
        own[...] = state_ref[:K] + got_ref[:K]
        if rest:
            rest[0][...] = state_ref[K:] + got_ref[K:]

    shapes = [(K, width)] + ([(rows - K, width)] if rows > K else [])
    return call_in_turn(body, [state, got], shapes, after, "sum_last")


def join(own, got, after):
    rows, width = own.shape

    def body(own_ref, got_ref, out):
        out[:rows] = own_ref[...]
        out[rows:] = got_ref[...]

    return call_in_turn(body, [own, got], [(2 * rows, width)], after, "join")[0]


def pass_on(value, after):
    any_space = pl.BlockSpec(memory_space=pl.ANY)
    return pl.pallas_call(
        lambda *refs: None,
        in_specs=[any_space] * 2,
        out_specs=any_space,
        out_shape=jax.ShapeDtypeStruct(value.shape, value.dtype),
        input_output_aliases={0: 0},
        compiler_params=pltpu.CompilerParams(vmem_limit_bytes=MIB),
        name="pass_on",
    )(value, after)


def put_products(pieces, arrays, inverse, out, ready, done):
    place, side = here()
    high, low = halves(inverse[...])
    wide = jnp.concatenate([high, high], axis=1)
    copies = []
    filled = [0, 0, 0]
    for array, (chain, other, first) in zip(arrays, pieces):
        owner = 1 - side if other else side
        width = WIDTH[chain]
        for i in range(2):
            value_high, value_low = halves(array[K * i : K * i + K])
            at = filled[chain]
            filled[chain] += 1
            stacked = jnp.concatenate([value_high, value_low], axis=0)
            ready[chain][at] = mul(wide, stacked) + mul(low, value_high)
            quarter = place[chain] ^ two_bits(QUARTERS, owner ^ FLIP[chain], first + i)
            column = pl.multiple_of(owner * HALF + STARTS[chain] + quarter * width, K)
            copies.append(
                pltpu.make_async_copy(ready[chain].at[at], out.at[:, pl.ds(column, width)], done.at[len(copies)])
            )
            copies[-1].start()
    return copies


def apply_first_kernel(pieces, scale, inverse, sampled, *rest):
    arrays, (out, basis, mark, *ready, basis_ready, done, basis_done) = rest[: len(pieces)], rest[len(pieces) :]
    mark[...] = jnp.zeros_like(mark)
    copies = put_products(pieces, arrays, inverse, out, ready, done)
    across_high, across_low = halves(inverse[...].T)
    high, low = halves(sampled[...])
    wide = jnp.concatenate([across_high, across_high], axis=0)
    basis_ready[...] = scale * (mul(jnp.concatenate([high, low], axis=1), wide) + mul(high, across_low))
    copies.append(pltpu.make_async_copy(basis_ready, basis, basis_done))
    copies[-1].start()
    for copy in copies:
        copy.wait()


def apply_next_kernel(pieces, inverse, *rest):
    arrays, (_, out, *ready, done) = rest[: len(pieces)], rest[len(pieces) :]
    for copy in put_products(pieces, arrays, inverse, out, ready, done):
        copy.wait()


def apply_scratch(pieces):
    most = [2 * sum(piece[0] == chain for piece in pieces) for chain in range(3)]
    return [pltpu.VMEM((most[chain], K, WIDTH[chain]), F32) for chain in range(3)]


def apply_first(inverse, parts, pieces, sampled, scale):
    return pl.pallas_call(
        lambda *refs: apply_first_kernel(pieces, scale, *refs),
        in_specs=[VMEM] * (2 + len(parts)),
        out_specs=[HBM, HBM, VMEM],
        out_shape=[
            jax.ShapeDtypeStruct((K, 2 * HALF), F32),
            jax.ShapeDtypeStruct(sampled.shape, F32),
            jax.ShapeDtypeStruct((8, K), F32),
        ],
        scratch_shapes=[
            *apply_scratch(pieces),
            pltpu.VMEM(sampled.shape, F32),
            pltpu.SemaphoreType.DMA((2 * len(pieces),)),
            pltpu.SemaphoreType.DMA,
        ],
        compiler_params=pltpu.CompilerParams(vmem_limit_bytes=12 * MIB),
        cost_estimate=pl.CostEstimate(flops=10**9, bytes_accessed=2 * MIB, transcendentals=0),
        name="apply_first",
    )(inverse, sampled, *parts)


def apply_next(inverse, parts, pieces, before):
    return pl.pallas_call(
        lambda *refs: apply_next_kernel(pieces, *refs),
        in_specs=[VMEM] * (1 + len(parts)) + [HBM],
        out_specs=HBM,
        out_shape=jax.ShapeDtypeStruct((K, 2 * HALF), F32),
        scratch_shapes=[*apply_scratch(pieces), pltpu.SemaphoreType.DMA((2 * len(pieces),))],
        input_output_aliases={1 + len(parts): 0},
        compiler_params=pltpu.CompilerParams(vmem_limit_bytes=12 * MIB),
        cost_estimate=pl.CostEstimate(flops=10**9, bytes_accessed=2 * MIB, transcendentals=0),
        name="apply_next",
    )(inverse, *parts, before)


def send(value, pairs):
    return lax.ppermute(value, AXES, pairs)


def per_device(slab, sketch):
    total_rows = slab.shape[0] * lax.axis_size("row") * lax.axis_size("col")
    turns = (0, 1, 2)
    sampled, left, sent_high, sent_low, high, low, first = sample(slab, sketch)
    sent = [first, *rest_to_send(left, sent_high, sent_low, first)]
    after = sent[2]
    kept, handed, states, near, far = [None] * 3, [None] * 3, [None] * 3, [None] * 3, [None] * 3
    cores = [None] * 3
    for chain in turns:
        cores[chain] = send(sent[chain], CORE_PAIRS)
        own = own_part(chain, (2, 3), left, high, low, sent[2] if chain == 2 else None, after)
        handed[chain] = after = sum_handed(own, cores[chain], None)
    for chain in turns:
        own = own_part(chain, (0, 1), left, high, low, None, after)
        kept[chain] = after = sum_kept(own, cores[chain], None)
    for chain in turns:
        got = send(handed[chain], ring_pairs(chain, 0, FLIP[chain]))
        kept[chain], handed[chain] = sum_half(kept[chain], handed[chain], got, after)
        after = kept[chain]
    for chain in turns:
        got = send(handed[chain], ring_pairs(chain, 1, FLIP[chain]))
        states[chain] = after = sum_half(kept[chain], handed[chain], got, after)
    for turn, step in ((1, 0), (1, 1), (2, 0)):
        for chain in turns:
            got = send(states[chain], ring_pairs((chain + turn) % 3, step, FLIP[chain]))
            states[chain] = after = sum_whole(states[chain], got, after)
    gram = None
    for chain in turns:
        got = send(states[chain], ring_pairs((chain + 2) % 3, 1, FLIP[chain]))
        states[chain], *rest = sum_last(states[chain], got, after)
        after = states[chain]
        gram = rest[0] if rest else gram
    state = [gram]
    for chain, panels in zip(turns, ((0, 2), (2, 4), (4, 5))):
        state = factor_part(state, panels, after)
        got = send(states[chain], ring_pairs(chain, 1, FLIP[chain]))
        near[chain] = after = join(states[chain], got, state[0])
    (inverse,) = factor_part(state, (5, 16), after)
    scale = math.sqrt(total_rows)
    out, basis, mark = apply_first(inverse, near, [(a, 0, 0) for a in range(3)], sampled, scale)
    near_other = [send(pass_on(part, mark), CORE_PAIRS) for part in near]
    for chain in turns:
        far[chain] = pass_on(send(near[chain], ring_pairs(chain, 0, FLIP[chain])), mark)
    far_other = [send(part, CORE_PAIRS) for part in far]
    middle = [(a, 0, 2) for a in range(3)] + [(a, 1, 0) for a in range(3)]
    out = apply_next(inverse, far + near_other, middle, out)
    out = apply_next(inverse, far_other, [(a, 1, 2) for a in range(3)], out)
    return basis, out


def solution(mesh):
    return jax.shard_map(
        per_device,
        mesh=mesh,
        in_specs=(P(AXES, None), P()),
        out_specs=(P(AXES, None), P()),
        check_vma=False,
    )
```
